256 devices in a mesh: gx: 4 (over z_hi, core), yz: 64 (over x, z_lo, y).
Axes of the slice: x: 4, y: 4, z: 8 (z_hi: 2, z_lo: 4; z = z_hi * 4 + z_lo), core: 2. Of those that a mesh axis runs over, the one named last changes fastest.
Arguments:
- hidden_in: bfloat16 [2, 256, 9216], P(None, 'yz', 'gx'), may hold values from -80 to 80
- norm_gain: float32 [9216], P('gx'), may hold values from 0.5 to 1.5
- w_qkv: bfloat16 [9216, 6656], P('gx', 'yz'), may hold values from -0.0625 to 0.0625
- w_gate: bfloat16 [9216, 36864], P('gx', 'yz'), may hold values from -0.0625 to 0.0625
- w_up: bfloat16 [9216, 36864], P('gx', 'yz'), may hold values from -0.0625 to 0.0625
- w_out: bfloat16 [6144, 9216], P('yz', 'gx'), may hold values from -0.078125 to 0.078125
- w_down: bfloat16 [36864, 9216], P('yz', 'gx'), may hold values from -0.03125 to 0.03125
- kv_cache: bfloat16 [256, 2048, 512], P(('gx', 'yz')), may hold values from -304 to 304
- lengths: int32 [256], P(('gx', 'yz')), may hold values from 1 to 2048, as said below
Outputs:
- layer_out: bfloat16 [2, 256, 9216], P(None, 'yz', 'gx')
The draws below stay inside these ranges and needn't reach their ends.
Inputs may be any that keep to these rules, and one draw needn't show every extreme that they name: `lengths`: every row has 1 to 2048 cached tokens; some row has exactly 2048 and some exactly 1.
All inputs are finite; a program needn't handle non-finite values.
Results may differ from the reference program's by a relative error of at most 0.009.
Values may be sent and summed in bfloat16 or wider, within the bound.
A program may use at most 64 MiB of HBM per device.

```python
import jax
import jax.numpy as jnp
from jax import lax

D = 9216
FF = 36864
HEADS = 24
HEAD_DIM = 256
CTX = 2048
STEPS = 2
BATCH = 256


def draw_hidden_in(key, part):
    key = jax.random.fold_in(key, 3)
    noise_key, scale_key = jax.random.split(key, 2)
    column = jnp.arange(D, dtype=jnp.float32)
    rising = 3.0 ** (column / D) * jax.random.uniform(scale_key, (D,), jnp.float32, 0.7, 1.4)
    values = jnp.clip(jax.random.normal(noise_key, (STEPS, BATCH, D), jnp.float32), -5.0, 5.0) * rising
    return values.astype(jnp.bfloat16)


def draw_kv_cache(key, part):
    key = jax.random.fold_in(key, 11)
    base_key = jax.random.fold_in(key, 0)
    cache = jnp.clip(jax.random.normal(base_key, (BATCH, CTX, 2 * HEAD_DIM), jnp.float32), -6.0, 6.0)
    return cache.astype(jnp.bfloat16)


def draw_lengths(key, part):
    key = jax.random.fold_in(key, 5)
    draw_key, pick_key = jax.random.split(key, 2)
    counts = jax.random.randint(draw_key, (BATCH,), 1, CTX + 1)
    order = jax.random.permutation(pick_key, BATCH)
    counts = counts.at[order[0]].set(CTX)
    counts = counts.at[order[1]].set(1)
    return counts.astype(jnp.int32)


def block_levels(stream_key, dims, pieces, smallest, largest):
    def one(dim, blocks):
        steps = jax.random.uniform(jax.random.fold_in(jax.random.fold_in(stream_key, 6), dim), (blocks,), jnp.float32, smallest / len(pieces), largest / len(pieces))
        return jnp.repeat(jnp.exp(steps), dims[dim] // blocks).reshape((-1,) + (1,) * (len(dims) - dim - 1))

    level = one(*pieces[0])
    for cut in pieces[1:]:
        level = level * one(*cut)
    return level


def bell_draw(own_key, extent, scale, bound, cuts=(), kind=jnp.bfloat16):
    drawn = scale * jax.random.normal(own_key, extent, jnp.float32)
    if cuts:
        drawn = drawn * block_levels(own_key, extent, cuts, -0.22, 0.18)
    return jnp.clip(drawn, -bound, bound).astype(kind)


def setup_inputs(seed: int = 0) -> dict:
    key_list = jax.random.split(jax.random.key(seed), 10)
    hidden_in = draw_hidden_in(jax.random.fold_in(key_list[9], 71), 0)
    norm_gain = jnp.clip(1.0 + 0.1 * jax.random.normal(key_list[1], (D,), jnp.float32), 0.5, 1.5)
    w_qkv = bell_draw(key_list[2], (D, (HEADS + 2) * HEAD_DIM), D ** -0.5, 0.0625, ((0, 4), (1, 64)))
    w_gate = bell_draw(key_list[3], (D, FF), D ** -0.5, 0.0625, ((0, 4), (1, 64)))
    w_up = bell_draw(key_list[4], (D, FF), D ** -0.5, 0.0625, ((0, 4), (1, 64)))
    w_out = bell_draw(key_list[5], (HEADS * HEAD_DIM, D), (HEADS * HEAD_DIM) ** -0.5, 0.078125, ((0, 64), (1, 4)))
    w_down = bell_draw(key_list[6], (FF, D), FF ** -0.5, 0.03125, ((0, 64), (1, 4)))
    kv_cache = draw_kv_cache(jax.random.fold_in(key_list[9], 71), 0)
    lengths = draw_lengths(jax.random.fold_in(key_list[9], 71), 0)
    return dict(hidden_in=hidden_in, norm_gain=norm_gain, w_qkv=w_qkv, w_gate=w_gate, w_up=w_up, w_out=w_out, w_down=w_down, kv_cache=kv_cache, lengths=lengths)


EPS = 1e-06
SCALE = 0.0625

def rotate(values, position):
    half = values.shape[-1] // 2
    freqs = 10000.0 ** (-jnp.arange(half, dtype=jnp.float32) / half)
    angle = position[..., None] * freqs
    cosine = jnp.cos(angle)
    sine = jnp.sin(angle)
    first = values[..., :half]
    second = values[..., half:]
    return jnp.concatenate([first * cosine - second * sine, second * cosine + first * sine], -1)

def layer_norm(layer_in, norm_gain):
    values = layer_in.astype(jnp.float32)
    mean = lax.optimization_barrier(jnp.mean(values, -1, keepdims=True))
    var = lax.optimization_barrier(jnp.mean(values * values, -1, keepdims=True)) - mean * mean
    return ((values - mean) * lax.rsqrt(var + EPS) * norm_gain).astype(jnp.bfloat16)

def attend_row(packed):
    queries, cache_row, length, keys_new, values_new = packed
    cached_keys = cache_row[:, :HEAD_DIM].astype(jnp.float32)
    cached_values = cache_row[:, HEAD_DIM:].astype(jnp.float32)
    query_f = queries.astype(jnp.float32)
    old_scores = jnp.einsum('hd,td->ht', query_f, cached_keys) * SCALE
    valid = jnp.arange(CTX)[None, :] < length
    old_scores = jnp.where(valid, old_scores, jnp.float32(-1e+30))
    new_scores = jnp.einsum('hd,nd->hn', query_f, keys_new.astype(jnp.float32)) * SCALE
    scores = jnp.concatenate([old_scores, new_scores], 1)
    peak = lax.optimization_barrier(jnp.max(scores, 1, keepdims=True))
    expd = jnp.exp(scores - peak)
    weights = (expd / lax.optimization_barrier(jnp.sum(expd, 1, keepdims=True))).astype(jnp.bfloat16).astype(jnp.float32)
    mixed = jnp.einsum('ht,td->hd', weights[:, :CTX], cached_values)
    mixed = mixed + jnp.einsum('hn,nd->hd', weights[:, CTX:], values_new.astype(jnp.float32))
    return mixed.reshape(HEADS * HEAD_DIM).astype(jnp.bfloat16)

def reference(hidden_in, norm_gain, w_qkv, w_gate, w_up, w_out, w_down, kv_cache, lengths):
    outputs = []
    keys_list = []
    values_list = []
    for step in range(STEPS):
        layer_in = hidden_in[step]
        normed = layer_norm(layer_in, norm_gain)
        qkv = jnp.dot(normed, w_qkv, preferred_element_type=jnp.float32).astype(jnp.bfloat16)
        position = lengths.astype(jnp.float32) + step
        query_part = qkv[:, :HEADS * HEAD_DIM].reshape(-1, HEADS, HEAD_DIM).astype(jnp.float32)
        queries = rotate(query_part, position[:, None]).astype(jnp.bfloat16)
        key_part = qkv[:, HEADS * HEAD_DIM:(HEADS + 1) * HEAD_DIM].astype(jnp.float32)
        keys_list.append(rotate(key_part, position).astype(jnp.bfloat16))
        values_list.append(qkv[:, (HEADS + 1) * HEAD_DIM:])
        attended = lax.map(attend_row, (queries, kv_cache, lengths, jnp.stack(keys_list, 1), jnp.stack(values_list, 1)))
        gate_part = jnp.dot(normed, w_gate, preferred_element_type=jnp.float32)
        up_part = jnp.dot(normed, w_up, preferred_element_type=jnp.float32)
        hidden = (jax.nn.silu(gate_part) * up_part).astype(jnp.bfloat16)
        total = jnp.dot(attended, w_out, preferred_element_type=jnp.float32)
        total = total + jnp.dot(hidden, w_down, preferred_element_type=jnp.float32)
        outputs.append((layer_in.astype(jnp.float32) + total).astype(jnp.bfloat16))
    return jnp.stack(outputs)
```

```python
import functools

import jax
import jax.numpy as jnp
from jax import lax
from jax.experimental import pallas as pl
from jax.experimental.pallas import tpu as pltpu
from jax.sharding import PartitionSpec as P

D = 9216
HEADS = 24
HEAD_DIM = 256
CTX = 2048
STEPS = 2
EPS = 1e-06
SCALE = 0.0625
WIDTH = 2304
HALF = 1152
UNITS = 576
QCOLS = 104
OCOLS = 96
MESH = pl.DeviceIdType.MESH
F32 = jnp.float32
BF16 = jnp.bfloat16


class Place:
    def __init__(self):
        g = lax.axis_index("gx")
        j = lax.axis_index("yz")
        self.g, self.j = g, j
        self.zh, self.c = g // 2, g % 2
        self.x, self.z, self.y = j // 16, (j // 4) % 4, j % 4

    def along_x(self, d):
        t = (self.x + d) % 4
        return t, (self.g, t * 16 + self.z * 4 + self.y)

    def along_z(self, d):
        t = (self.z + d) % 4
        return t, (self.g, self.x * 16 + t * 4 + self.y)

    def along_y(self, d):
        t = (self.y + d) % 4
        return t, (self.g, self.x * 16 + self.z * 4 + t)

    def other_core(self):
        return (self.zh * 2 + (1 - self.c), self.j)

    def other_half(self):
        return ((1 - self.zh) * 2 + self.c, self.j)

    def gx_partner(self, d):
        return ((self.g + d) % 4, self.j)


def greet(me):
    barrier = pltpu.get_barrier_semaphore()
    for d in (1, 2, 3):
        for target in (me.along_x(d)[1], me.along_z(d)[1], me.along_y(d)[1], me.gx_partner(d)):
            pl.semaphore_signal(barrier, inc=1, device_id=target, device_id_type=MESH)
    pl.semaphore_wait(barrier, 12)


class Wire:
    def __init__(self, send_sems, recv_sems):
        self.send_sems, self.recv_sems = send_sems, recv_sems
        self.used = 0
        self.open = []

    def send(self, src, dst, target):
        copy = pltpu.make_async_remote_copy(
            src_ref=src,
            dst_ref=dst,
            send_sem=self.send_sems.at[self.used],
            recv_sem=self.recv_sems.at[self.used],
            device_id=target,
            device_id_type=MESH,
        )
        self.used += 1
        copy.start()
        self.open.append(copy)
        return copy

    def close(self):
        for copy in self.open:
            copy.wait_send()


def arrive(copies):
    for copy in copies:
        copy.wait_recv()


def dot(a, b):
    return jnp.dot(a, b, preferred_element_type=F32)


def dot_t(a, b):
    return lax.dot_general(a, b, (((1,), (1,)), ((), ())), preferred_element_type=F32)


def normalise(me, wire, hidden_ref, gain_ref, stats, shard):
    rows = jnp.concatenate([hidden_ref[0].astype(F32), hidden_ref[1].astype(F32)], 0)
    stats[3, 0] = jnp.broadcast_to(jnp.sum(rows, 1, keepdims=True), (8, 128))
    stats[3, 1] = jnp.broadcast_to(jnp.sum(rows * rows, 1, keepdims=True), (8, 128))
    arrive([wire.send(stats.at[3], stats.at[d - 1], me.gx_partner(d)) for d in (1, 2, 3)])
    total = (stats[0] + stats[1]) + (stats[2] + stats[3])
    mean = total[0, :, :1] / D
    var = total[1, :, :1] / D - mean * mean
    normed = (rows - mean) * lax.rsqrt(var + EPS) * gain_ref[...]
    shard[...] = jnp.concatenate([normed[:, :HALF], normed[:, HALF:]], 0).astype(BF16)


def gather_rows(me, wire, every):
    own = every.at[me.x, me.z, me.y]
    arrive([wire.send(own, own, me.along_z(d)[1]) for d in (1, 2, 3)])
    low = every.at[me.x, pl.ds(0, 2), me.y]
    high = every.at[me.x, pl.ds(2, 2), me.y]
    copies = []
    for d in (1, 2, 3):
        copies.append(wire.send(low, low, me.along_x(d)[1]))
        copies.append(wire.send(high, high, me.along_y(d)[1]))
    arrive(copies)
    low = every.at[:, pl.ds(0, 2), me.y]
    high = every.at[me.x, pl.ds(2, 2)]
    copies = []
    for d in (1, 2, 3):
        copies.append(wire.send(low, low, me.along_y(d)[1]))
        copies.append(wire.send(high, high, me.along_x(d)[1]))
    arrive(copies)


def unfold(every, normed):
    def body(i, _):
        block = every[i // 4, i % 4].astype(F32)
        rows = pl.ds(pl.multiple_of(i * 32, 32), 32)
        normed[rows, :HALF] = block[:, :8].reshape(32, HALF).astype(BF16)
        normed[rows, HALF:] = block[:, 8:].reshape(32, HALF).astype(BF16)
        return 0

    lax.fori_loop(0, 16, body, 0)


def first_products(me, m, normed, wq, wg, wu, qkv, gu):
    rows = normed[pl.ds(pl.multiple_of(m * 256, 256), 256), :]
    part = dot_t(rows, wq[...]).astype(BF16)
    gate = dot_t(rows, wg[...])
    up = dot_t(rows, wu[...])
    tail = jnp.concatenate([gate[:, 512:], up[:, 512:]], 1)
    for c in (0, 1):
        own = slice(128 * c, 128 * c + 128)
        qkv[m, c] = jnp.concatenate([part[own], jnp.zeros((128, 24), BF16)], 1)
        gu[m, c, :, :512] = gate[own, :512].astype(BF16)
        gu[m, c, :, 512:1024] = up[own, :512].astype(BF16)
        gu[m, c, :, 1024:] = tail[own].astype(BF16)


def add_into(out, a, b, rows=32):
    def body(i, _):
        at = pl.ds(pl.multiple_of(i * rows, rows), rows)
        out[at, :] = (a[at, :].astype(F32) + b[at, :].astype(F32)).astype(BF16)
        return 0

    lax.fori_loop(0, 128 // rows, body, 0)


def reduce_width(me, wire, normed, wq, wg, wu, qkv, gu, qkv_in, gu_in, qkv_far, gu_far):
    far = 1 - me.zh
    for m in (far, me.zh):
        first_products(me, m, normed, wq, wg, wu, qkv, gu)
        near = [
            wire.send(qkv.at[m, 1 - me.c], qkv_in.at[m], me.other_core()),
            wire.send(gu.at[m, 1 - me.c], gu_in.at[m], me.other_core()),
        ]
        arrive(near)
        add_into(qkv.at[m, me.c], qkv.at[m, me.c], qkv_in.at[m])
        if m is far:
            qkv_copy = wire.send(qkv.at[m, me.c], qkv_far, me.other_half())
        add_into(gu.at[m, me.c], gu.at[m, me.c], gu_in.at[m])
        if m is far:
            gu_copy = wire.send(gu.at[m, me.c], gu_far, me.other_half())
    return qkv_copy, gu_copy


def spread_qkv(me, wire, share, r1, q2, r2, r3):
    copies = []
    for d in (1, 2, 3):
        t, target = me.along_x(d)
        copies.append(wire.send(share.at[t], r1.at[me.x], target))
    r1[me.x] = share[me.x]
    arrive(copies)
    mixed = r1[...].astype(F32).reshape(4, 4, 8, 128)
    for t in range(4):
        q2[t] = mixed[:, t].reshape(32, 128).astype(BF16)
    copies = []
    for d in (1, 2, 3):
        t, target = me.along_z(d)
        copies.append(wire.send(q2.at[t], r2.at[me.z], target))
    r2[me.z] = q2[me.z]
    arrive(copies)
    copies = [wire.send(r2, r3.at[me.y], me.along_y(d)[1]) for d in (1, 2, 3)]
    r3[me.y] = r2[...]
    arrive(copies)
    row = lax.broadcasted_iota(jnp.int32, (128, 512), 0)
    col = lax.broadcasted_iota(jnp.int32, (128, 512), 1)
    wanted = (
        ((col >> 3) & 3) * 32
        + ((col >> 5) & 3) * 8
        + ((col >> 7) & 3) * 2
        + ((col >> 2) & 1)
    )
    pick = jnp.where((row == wanted) & ((col & 3) == me.y), 1.0, 0.0).astype(BF16)
    return dot(pick, r3[...].reshape(512, 128))


def collect_heads(me, wire, t_ref, r1, q2, r2, r3):
    copies = []
    for d in (1, 2, 3):
        t, target = me.along_x(d)
        copies.append(wire.send(t_ref.at[t], r1.at[me.x], target))
    r1[me.x] = t_ref[me.x]
    arrive(copies)
    mixed = r1[...].astype(F32).reshape(4, 4, 8, 128)
    for t in range(4):
        q2[t] = mixed[:, t].reshape(32, 128).astype(BF16)
    copies = []
    for d in (1, 2, 3):
        t, target = me.along_z(d)
        copies.append(wire.send(q2.at[t], r2.at[me.z], target))
    r2[me.z] = q2[me.z]
    arrive(copies)
    copies = [wire.send(r2, r3.at[me.y], me.along_y(d)[1]) for d in (1, 2, 3)]
    r3[me.y] = r2[...]
    arrive(copies)
    row = lax.broadcasted_iota(jnp.int32, (128, 512), 0)
    col = lax.broadcasted_iota(jnp.int32, (128, 512), 1)
    wanted = (
        ((col >> 3) & 3) * 32
        + ((col >> 5) & 3) * 8
        + (col & 1) * 4
        + ((col >> 7) & 3)
    )
    pick = jnp.where((row == wanted) & (((col >> 1) & 3) == me.y), 1.0, 0.0).astype(BF16)
    return dot(pick, r3[...].reshape(512, 128)).astype(BF16)


def share_blocks(me, wire, blocks):
    own = blocks.at[me.zh, me.c]
    arrive([wire.send(own, own, me.other_half())])
    pair = blocks.at[:, me.c]
    arrive([wire.send(pair, pair, me.other_core())])


def activate(gu, gu_far, out):
    def body(i, _):
        at = pl.ds(pl.multiple_of(i * 32, 32), 32)
        total = gu[at, :].astype(F32) + gu_far[at, :].astype(F32)
        gate, up = total[:, :512], total[:, 512:1024]
        out[at, :512] = (gate / (1.0 + jnp.exp(-gate)) * up).astype(BF16)
        tail = total[:, 1024:]
        last = tail / (1.0 + jnp.exp(-tail)) * pltpu.roll(tail, 64, 1)
        lane = lax.broadcasted_iota(jnp.int32, last.shape, 1)
        out[at, 512:] = jnp.where(lane < 64, last, 0.0).astype(BF16)
        return 0

    lax.fori_loop(0, 4, body, 0)


def kernel_one(
    hidden_ref, gain_ref, wq, wg, wu, qkv_out, hidden_out,
    stats, every, normed, qkv, gu, qkv_in, gu_in, qkv_far, gu_far, share, r1, q2, r2, r3, blocks,
    send_sems, recv_sems,
):
    me = Place()
    wire = Wire(send_sems, recv_sems)
    greet(me)
    normalise(me, wire, hidden_ref, gain_ref, stats, every.at[me.x, me.z, me.y])
    gather_rows(me, wire, every)
    unfold(every, normed)
    qkv_copy, gu_copy = reduce_width(
        me, wire, normed, wq, wg, wu, qkv, gu, qkv_in, gu_in, qkv_far, gu_far
    )
    arrive([qkv_copy])
    whole = qkv[me.zh, me.c].astype(F32) + qkv_far[...].astype(F32)
    share[...] = whole.astype(BF16).reshape(4, 32, 128)
    qkv_out[...] = spread_qkv(me, wire, share, r1, q2, r2, r3)
    arrive([gu_copy])
    activate(gu.at[me.zh, me.c], gu_far, blocks.at[me.zh, me.c])
    share_blocks(me, wire, blocks)
    hidden_out[...] = blocks[...]
    wire.close()


def kernel_attend(lengths_ref, qkv_ref, cache_ref, out_ref, flat, heads, fresh_k, fresh_v, flat_out):
    for j in range(64):
        flat[:, QCOLS * j : QCOLS * j + QCOLS] = qkv_ref[2 * j : 2 * j + 2, :QCOLS]
    for h in range(HEADS + 1):
        heads[2 * h : 2 * h + 2, :] = flat[:, 256 * h : 256 * h + 256]
    length = lengths_ref[0]
    count = 2 * HEADS + 8
    row = lax.broadcasted_iota(jnp.int32, (count, 1), 0)
    lane = lax.broadcasted_iota(jnp.int32, (8, 128), 1).astype(F32)
    freqs = 10000.0 ** (-lane / 128.0)
    step8 = (lax.broadcasted_iota(jnp.int32, (8, 128), 0) & 1).astype(F32)
    angle = (length.astype(F32) + step8) * freqs
    cosine = jnp.cos(angle)
    sine = jnp.sin(angle)
    cosine = jnp.concatenate([cosine] * (count // 8), 0)
    sine = jnp.concatenate([sine] * (count // 8), 0)
    first, second = heads[:count, :128], heads[:count, 128:]
    turned = jnp.concatenate(
        [first * cosine - second * sine, second * cosine + first * sine], 1
    )
    queries = turned[: 2 * HEADS].astype(BF16)
    in_use = lax.broadcasted_iota(jnp.int32, (16, 256), 0) < 2
    fresh_k[...] = jnp.where(
        in_use, jnp.concatenate([turned[2 * HEADS :], turned[2 * HEADS :]], 0), 0.0
    ).astype(BF16)
    fresh_v[...] = jnp.zeros((16, 256), F32)
    fresh_v[0:2, :] = flat[:, 6400:6656]
    keys = cache_ref[0, :, :256]
    values = cache_ref[0, :, 256:]
    old = dot_t(queries, keys) * SCALE
    slot = lax.broadcasted_iota(jnp.int32, old.shape, 1)
    old = jnp.where(slot < length, old, -1e30)
    new = dot_t(queries, fresh_k[...]) * SCALE
    new_slot = lax.broadcasted_iota(jnp.int32, new.shape, 1)
    new_step = lax.broadcasted_iota(jnp.int32, new.shape, 0) & 1
    new = jnp.where(new_slot <= new_step, new, -1e30)
    peak = jnp.maximum(jnp.max(old, 1, keepdims=True), jnp.max(new, 1, keepdims=True))
    old = jnp.exp(old - peak)
    new = jnp.exp(new - peak)
    total = jnp.sum(old, 1, keepdims=True) + jnp.sum(new, 1, keepdims=True)
    mixed = dot((old / total).astype(BF16), values) + dot(
        (new / total).astype(BF16), fresh_v[...].astype(BF16)
    )
    heads[: 2 * HEADS, :] = mixed
    for h in range(HEADS):
        flat_out[:, 256 * h : 256 * h + 256] = heads[2 * h : 2 * h + 2, :]
    out_ref[...] = jnp.zeros((128, 128), F32)
    for j in range(64):
        out_ref[2 * j : 2 * j + 2, :OCOLS] = flat_out[:, OCOLS * j : OCOLS * j + OCOLS]


def second_products(hidden, heads, wo, wd, partial):
    def body(m, _):
        lines = hidden[m].reshape(256, 640)
        attended = heads[m].reshape(256, 128)[:, :OCOLS]
        for n in range(0, HALF, 384):
            sides = []
            for at in (n, HALF + n):
                columns = slice(at, at + 384)
                product = (
                    dot(lines[:, :512], wd[:512, columns])
                    + dot(lines[:, 512:UNITS], wd[512:, columns])
                    + dot(attended, wo[:, columns])
                )
                sides.append(product.reshape(2, 4, 4, 8, 384))
            partial[pl.ds(m * 2, 2), :, :, :, n : n + 384] = jnp.concatenate(sides, 3).astype(BF16)
        return 0

    lax.fori_loop(0, 2, body, 0)


def scatter_rows(me, wire, partial, ra, rb, sa, sb, ra2, rb2, sz, rz):
    copies = []
    for d in (1, 2, 3):
        t, target = me.along_y(d)
        copies.append(wire.send(partial.at[:, pl.ds(0, 2), t], ra.at[d - 1], target))
        t, target = me.along_x(d)
        copies.append(wire.send(partial.at[t, pl.ds(2, 2)], rb.at[d - 1], target))
    arrive(copies)

    def add_low(i, _):
        total = partial[i, pl.ds(0, 2), me.y].astype(F32)
        for d in range(3):
            total = total + ra[d, i].astype(F32)
        sa[i] = total.astype(BF16)
        return 0

    lax.fori_loop(0, 4, add_low, 0)

    def add_high(i, _):
        total = partial[me.x, 2 + i // 2, pl.ds((i % 2) * 2, 2)].astype(F32)
        for d in range(3):
            total = total + rb[d, i // 2, pl.ds((i % 2) * 2, 2)].astype(F32)
        sb[i // 2, pl.ds((i % 2) * 2, 2)] = total.astype(BF16)
        return 0

    lax.fori_loop(0, 4, add_high, 0)
    copies = []
    for d in (1, 2, 3):
        t, target = me.along_x(d)
        copies.append(wire.send(sa.at[t], ra2.at[d - 1], target))
        t, target = me.along_y(d)
        copies.append(wire.send(sb.at[:, t], rb2.at[d - 1], target))
    arrive(copies)
    low = sa[me.x].astype(F32)
    high = sb[:, me.y].astype(F32)
    for d in range(3):
        low = low + ra2[d].astype(F32)
        high = high + rb2[d].astype(F32)
    sz[0:2] = low.astype(BF16)
    sz[2:4] = high.astype(BF16)
    copies = []
    for d in (1, 2, 3):
        t, target = me.along_z(d)
        copies.append(wire.send(sz.at[t], rz.at[d - 1], target))
    arrive(copies)
    total = sz[me.z].astype(F32)
    for d in range(3):
        total = total + rz[d].astype(F32)
    return total


def finish(hidden_ref, total, out_ref):
    whole = jnp.concatenate([total[:8], total[8:]], 1)
    for step in range(STEPS):
        rows = whole[4 * step : 4 * step + 4]
        out_ref[step] = (hidden_ref[step].astype(F32) + rows).astype(BF16)


def kernel_two(
    hidden_ref, heads_ref, lines, wo, wd, out_ref,
    t_ref, r1, q2, r2, r3, heads, partial, ra, rb, sa, sb, ra2, rb2, sz, rz,
    send_sems, recv_sems,
):
    me = Place()
    wire = Wire(send_sems, recv_sems)
    greet(me)
    t_ref[...] = heads_ref[...].astype(BF16).reshape(4, 32, 128)
    heads[me.zh, me.c] = collect_heads(me, wire, t_ref, r1, q2, r2, r3)
    share_blocks(me, wire, heads)
    second_products(lines, heads, wo, wd, partial)
    total = scatter_rows(me, wire, partial, ra, rb, sa, sb, ra2, rb2, sz, rz)
    finish(hidden_ref, total, out_ref)
    wire.close()


VM = pl.BlockSpec(memory_space=pltpu.VMEM)
A2A_SCRATCH = [
    pltpu.VMEM((4, 32, 128), BF16),
    pltpu.VMEM((4, 32, 128), BF16),
    pltpu.VMEM((4, 32, 128), BF16),
    pltpu.VMEM((4, 32, 128), BF16),
    pltpu.VMEM((4, 4, 32, 128), BF16),
]


def per_device(hidden_in, norm_gain, w_qkv, w_gate, w_up, w_out, w_down, kv_cache, lengths):
    qkv, hidden = pl.pallas_call(
        kernel_one,
        name="first_half",
        out_shape=(
            jax.ShapeDtypeStruct((128, 128), F32),
            jax.ShapeDtypeStruct((2, 2, 128, 640), BF16),
        ),
        in_specs=[VM] * 5,
        out_specs=(VM, VM),
        scratch_shapes=[
            pltpu.VMEM((4, 2, 8, 128), F32),
            pltpu.VMEM((4, 4, 4, 16, HALF), BF16),
            pltpu.VMEM((512, WIDTH), BF16),
            pltpu.VMEM((2, 2, 128, 128), BF16),
            pltpu.VMEM((2, 2, 128, 2 * UNITS), BF16),
            pltpu.VMEM((2, 128, 128), BF16),
            pltpu.VMEM((2, 128, 2 * UNITS), BF16),
            pltpu.VMEM((128, 128), BF16),
            pltpu.VMEM((128, 2 * UNITS), BF16),
        ]
        + A2A_SCRATCH
        + [
            pltpu.VMEM((2, 2, 128, 640), BF16),
            pltpu.SemaphoreType.DMA((40,)),
            pltpu.SemaphoreType.DMA((40,)),
        ],
        compiler_params=pltpu.CompilerParams(
            collective_id=0, has_side_effects=True, vmem_limit_bytes=48 * 2**20
        ),
    )(hidden_in, norm_gain.reshape(1, WIDTH), w_qkv.T, w_gate.T, w_up.T)
    heads = pl.pallas_call(
        kernel_attend,
        name="attend",
        out_shape=jax.ShapeDtypeStruct((128, 128), F32),
        in_specs=[pl.BlockSpec(memory_space=pltpu.SMEM), VM, VM],
        out_specs=VM,
        scratch_shapes=[
            pltpu.VMEM((2, 6656), F32),
            pltpu.VMEM((56, 256), F32),
            pltpu.VMEM((16, 256), BF16),
            pltpu.VMEM((16, 256), F32),
            pltpu.VMEM((2, 6144), F32),
        ],
        compiler_params=pltpu.CompilerParams(vmem_limit_bytes=32 * 2**20),
    )(lengths, qkv, kv_cache)
    return pl.pallas_call(
        kernel_two,
        name="second_half",
        out_shape=jax.ShapeDtypeStruct((2, 4, WIDTH), BF16),
        in_specs=[VM] * 5,
        out_specs=VM,
        scratch_shapes=A2A_SCRATCH
        + [
            pltpu.VMEM((2, 2, 128, 128), BF16),
            pltpu.VMEM((4, 4, 4, 16, HALF), BF16),
            pltpu.VMEM((3, 4, 2, 16, HALF), BF16),
            pltpu.VMEM((3, 2, 4, 16, HALF), BF16),
            pltpu.VMEM((4, 2, 16, HALF), BF16),
            pltpu.VMEM((2, 4, 16, HALF), BF16),
            pltpu.VMEM((3, 2, 16, HALF), BF16),
            pltpu.VMEM((3, 2, 16, HALF), BF16),
            pltpu.VMEM((4, 16, HALF), BF16),
            pltpu.VMEM((3, 16, HALF), BF16),
            pltpu.SemaphoreType.DMA((40,)),
            pltpu.SemaphoreType.DMA((40,)),
        ],
        compiler_params=pltpu.CompilerParams(
            collective_id=1, has_side_effects=True, vmem_limit_bytes=48 * 2**20
        ),
    )(hidden_in, heads, hidden, w_out, w_down)


def solution(mesh):
    return jax.shard_map(
        per_device,
        mesh=mesh,
        in_specs=(
            P(None, "yz", "gx"),
            P("gx"),
            P("gx", "yz"),
            P("gx", "yz"),
            P("gx", "yz"),
            P("yz", "gx"),
            P("yz", "gx"),
            P(("gx", "yz"), None, None),
            P(("gx", "yz")),
        ),
        out_specs=P(None, "yz", "gx"),
        check_vma=False,
    )
```

```python
import jax
import jax.numpy as jnp
from jax import lax
from jax.experimental import pallas as pl
from jax.experimental.pallas import tpu as pltpu
from jax.sharding import PartitionSpec as P

D = 9216
HEADS = 24
HEAD_DIM = 256
CTX = 2048
STEPS = 2
EPS = 1e-06
SCALE = 0.0625
WIDTH = 2304
HALF = 1152
UNITS = 576
QCOLS = 104
OCOLS = 96
MESH = pl.DeviceIdType.MESH
F32 = jnp.float32
BF16 = jnp.bfloat16


class Place:
    def __init__(self):
        g = lax.axis_index("gx")
        j = lax.axis_index("yz")
        self.g, self.j = g, j
        self.zh, self.c = g // 2, g % 2
        self.x, self.z, self.y = j // 16, (j // 4) % 4, j % 4

    def at(self, zh=0, c=0, x=0, z=0, y=0):
        g = ((self.zh + zh) % 2) * 2 + (self.c + c) % 2
        j = ((self.x + x) % 4) * 16 + ((self.z + z) % 4) * 4 + (self.y + y) % 4
        return (g, j)


def greet(me):
    barrier = pltpu.get_barrier_semaphore()
    count = 0
    for d in (1, 2, 3):
        partners = [me.at(x=d), me.at(z=d), me.at(y=d), me.at(c=1, x=d), me.at(zh=1, z=d)]
        partners.append(me.at(zh=d // 2, c=d % 2))
        for target in partners:
            pl.semaphore_signal(barrier, inc=1, device_id=target, device_id_type=MESH)
            count += 1
    pl.semaphore_wait(barrier, count)


class Wire:
    def __init__(self, send_sems, recv_sems):
        self.send_sems, self.recv_sems = send_sems, recv_sems
        self.used = 0
        self.open = []

    def send(self, src, dst, target):
        copy = pltpu.make_async_remote_copy(
            src_ref=src,
            dst_ref=dst,
            send_sem=self.send_sems.at[self.used],
            recv_sem=self.recv_sems.at[self.used],
            device_id=target,
            device_id_type=MESH,
        )
        self.used += 1
        copy.start()
        self.open.append(copy)
        return copy

    def close(self):
        for copy in self.open:
            copy.wait_send()


def arrive(copies):
    for copy in copies:
        copy.wait_recv()


def dot(a, b):
    return jnp.dot(a, b, preferred_element_type=F32)


def dot_t(a, b):
    return lax.dot_general(a, b, (((1,), (1,)), ((), ())), preferred_element_type=F32)


def fold(hidden, own, stats):
    rows = jnp.concatenate([hidden[0].astype(F32), hidden[1].astype(F32)], 0)
    own[...] = jnp.concatenate([rows[:, :HALF], rows[:, HALF:]], 0).astype(BF16)
    stats[0, 0] = jnp.broadcast_to(jnp.sum(rows, 1, keepdims=True), (8, 128))
    stats[0, 1] = jnp.broadcast_to(jnp.sum(rows * rows, 1, keepdims=True), (8, 128))


def moments(stats):
    total = (stats[0] + stats[1]) + (stats[2] + stats[3])
    mean = total[0] / D
    var = total[1] / D - mean * mean
    lane = lax.broadcasted_iota(jnp.int32, (8, 128), 1)
    return jnp.where(lane < 64, mean, lax.rsqrt(var + EPS))


def normalise(me, p, every, known, gain, normed):
    def body(i, _):
        z = (me.z + 2 * p + i // 4) % 4
        block = every[z, i % 4].astype(F32)
        about = known[i % 4, z].reshape(32, 128)
        mean, scale = about[:, :1], about[:, 64:65]
        left = (block[:, :8].reshape(32, HALF) - mean) * scale * gain[:, :HALF]
        right = (block[:, 8:].reshape(32, HALF) - mean) * scale * gain[:, HALF:]
        rows = pl.ds(pl.multiple_of(p * 256 + i * 32, 32), 32)
        normed[rows, :HALF] = left.astype(BF16)
        normed[rows, HALF:] = right.astype(BF16)
        return 0

    lax.fori_loop(0, 8, body, 0)


def qkv_products(p, normed, wq, qkv):
    part = dot_t(normed[256 * p : 256 * p + 256, :], wq[...])
    part = jnp.concatenate([part, jnp.zeros((256, 24), F32)], 1)
    qkv[2 * p : 2 * p + 2] = part.reshape(2, 2, 2, 32, 128).astype(BF16)


def gate_up_products(p, normed, wg, wu, gu):
    rows = normed[256 * p : 256 * p + 256, :]
    gate = dot_t(rows, wg[...])
    up = dot_t(rows, wu[...])
    tail = jnp.concatenate([gate[:, 512:], up[:, 512:]], 1)
    own = slice(2 * p, 2 * p + 2)
    gu[own, :, :, :, :512] = gate[:, :512].reshape(2, 2, 2, 32, 512).astype(BF16)
    gu[own, :, :, :, 512:1024] = up[:, :512].reshape(2, 2, 2, 32, 512).astype(BF16)
    gu[own, :, :, :, 1024:] = tail.reshape(2, 2, 2, 32, 128).astype(BF16)


def add_cores(me, p, half, gu, gu_in, gu_sum):
    def body(e, _):
        total = gu[2 * p + e, half, me.c].astype(F32) + gu_in[p, e, half].astype(F32)
        gu_sum[p, half, e] = total.astype(BF16)
        return 0

    lax.fori_loop(0, 2, body, 0)


def activate(me, p, gu_sum, gu_far, blocks):
    def body(e, _):
        total = gu_sum[p, me.zh, e].astype(F32) + gu_far[p, e].astype(F32)
        gate, up = total[:, :512], total[:, 512:1024]
        tail = total[:, 1024:]
        last = tail / (1.0 + jnp.exp(-tail)) * pltpu.roll(tail, 64, 1)
        lane = lax.broadcasted_iota(jnp.int32, last.shape, 1)
        blocks[2 * p + e, me.zh, me.c, :, :512] = (gate / (1.0 + jnp.exp(-gate)) * up).astype(BF16)
        blocks[2 * p + e, me.zh, me.c, :, 512:] = jnp.where(lane < 64, last, 0.0).astype(BF16)
        return 0

    lax.fori_loop(0, 2, body, 0)


def two_way(me, wire, along, other, piece, landing):
    copies = []
    for b in (0, 1):
        for d in range(4):
            if b or d:
                target = me.at(**{other: b, along: d})
                copies.append(wire.send(piece(b, d), landing.at[b, getattr(me, along)], target))
    return copies


def attend(length, g_ref, cache, t_ref, flat, heads, fresh_v, flat_out, t_wide):
    for j in range(64):
        flat[:, QCOLS * j : QCOLS * j + QCOLS] = g_ref[2 * j : 2 * j + 2, :QCOLS]
    heads[48:56, :] = jnp.zeros((8, 256), F32)
    for h in range(HEADS + 1):
        heads[2 * h : 2 * h + 2, :] = flat[:, 256 * h : 256 * h + 256]
    lane = lax.broadcasted_iota(jnp.int32, (8, 128), 1).astype(F32)
    freqs = 10000.0 ** (-lane / 128.0)
    step8 = (lax.broadcasted_iota(jnp.int32, (8, 128), 0) & 1).astype(F32)
    angle = (length.astype(F32) + step8) * freqs
    cosine = jnp.concatenate([jnp.cos(angle)] * 7, 0)
    sine = jnp.concatenate([jnp.sin(angle)] * 7, 0)
    first, second = heads[:, :128], heads[:, 128:]
    turned = jnp.concatenate(
        [first * cosine - second * sine, second * cosine + first * sine], 1
    )
    queries = turned[: 2 * HEADS].astype(BF16)
    fresh = turned[2 * HEADS :]
    fresh_k = jnp.concatenate([fresh, jnp.zeros((8, 256), F32)], 0).astype(BF16)
    fresh_v[...] = jnp.zeros((16, 256), F32)
    fresh_v[0:2, :] = flat[:, 6400:6656]
    keys = cache[0, :, :256]
    values = cache[0, :, 256:]
    old = dot_t(queries, keys) * SCALE
    slot = lax.broadcasted_iota(jnp.int32, old.shape, 1)
    old = jnp.where(slot < length, old, -1e30)
    new = dot_t(queries, fresh_k) * SCALE
    new_slot = lax.broadcasted_iota(jnp.int32, new.shape, 1)
    new_step = lax.broadcasted_iota(jnp.int32, new.shape, 0) & 1
    new = jnp.where(new_slot <= new_step, new, -1e30)
    peak = jnp.maximum(jnp.max(old, 1, keepdims=True), jnp.max(new, 1, keepdims=True))
    old = jnp.exp(old - peak)
    new = jnp.exp(new - peak)
    total = jnp.sum(old, 1, keepdims=True) + jnp.sum(new, 1, keepdims=True)
    mixed = dot((old / total).astype(BF16), values) + dot(
        (new / total).astype(BF16), fresh_v[...].astype(BF16)
    )
    heads[: 2 * HEADS, :] = mixed
    for h in range(HEADS):
        flat_out[:, 256 * h : 256 * h + 256] = heads[2 * h : 2 * h + 2, :]
    t_wide[...] = jnp.zeros((128, 128), F32)
    for j in range(64):
        t_wide[2 * j : 2 * j + 2, :OCOLS] = flat_out[:, OCOLS * j : OCOLS * j + OCOLS]
    t_ref[...] = t_wide[...].astype(BF16).reshape(4, 32, 128)


def write_picks(me, pick_in, pick_mid, pick_out):
    def write(pick, wanted, keep):
        rows, depth = pick.shape
        row = lax.broadcasted_iota(jnp.int32, (64, depth), 0)
        col = lax.broadcasted_iota(jnp.int32, (64, depth), 1)
        place = jnp.where(keep(col), wanted(col), -1)

        def body(i, _):
            at = pl.ds(pl.multiple_of(i * 64, 64), 64)
            pick[at, :] = jnp.where(row + i * 64 == place, 1.0, 0.0).astype(BF16)
            return 0

        lax.fori_loop(0, rows // 64, body, 0)

    def bits(k, low, count):
        return (k >> low) & ((1 << count) - 1)

    def arrived(k):
        return bits(k, 3, 2) * 32 + bits(k, 5, 2) * 8 + bits(k, 7, 2) * 2 + bits(k, 2, 1)

    def sorted_by_y(k):
        return (
            bits(k, 1, 2) * 128 + bits(k, 8, 1) * 64 + bits(k, 5, 1) * 32
            + bits(k, 6, 2) * 8 + bits(k, 3, 2) * 2 + bits(k, 0, 1)
        )

    def by_row(k):
        chunk = (bits(k, 1, 2) - me.z) & 3
        block = ((bits(k, 6, 1) + me.zh) & 1) * 2 + ((bits(k, 5, 1) + me.c) & 1)
        return chunk * 128 + block * 32 + bits(k, 3, 2) * 8 + bits(k, 0, 1) * 4 + bits(k, 7, 2)

    write(pick_in, arrived, lambda k: bits(k, 0, 2) == me.y)
    write(pick_mid, sorted_by_y, lambda k: k >= 0)
    write(pick_out, by_row, lambda k: k >= 0)


def second_products(p, blocks, heads, wo, wd, partial):
    lines = blocks[2 * p : 2 * p + 2].reshape(256, 640)
    attended = heads[256 * p : 256 * p + 256, :OCOLS]
    for n in range(0, HALF, 384):
        sides = []
        for at in (n, HALF + n):
            columns = slice(at, at + 384)
            product = (
                dot(lines[:, :512], wd[:512, columns])
                + dot(lines[:, 512:UNITS], wd[512:, columns])
                + dot(attended, wo[:, columns])
            )
            sides.append(product.reshape(2, 4, 4, 8, 384))
        partial[2 * p : 2 * p + 2, :, :, :, n : n + 384] = jnp.concatenate(sides, 3).astype(BF16)


def kernel(
    lengths_ref, hidden_hbm, gain_hbm, wq_hbm, wg_hbm, wu_hbm, wo_hbm, wd_hbm, cache_hbm, out_ref,
    hidden, gain, wq, wg, wu, wo, wd, cache, load_sems,
    stats, known, every, normed, qkv, gu, gu_in, gu_sum, gu_far, blocks,
    s1, q2, s2, s2_sum, s3, g_ref, t_ref, flat, heads32, fresh_v, flat_out, t_wide,
    u1, u1_sorted, u2, u2_sorted, u3, heads, pick_in, pick_mid, pick_out,
    partial, ra, sa, rb, sz, rz,
    send_sems, recv_sems,
):
    me = Place()
    wire = Wire(send_sems, recv_sems)
    loads = []
    for i, (src, dst) in enumerate(
        (
            (hidden_hbm, hidden), (gain_hbm, gain), (wq_hbm, wq), (wg_hbm, wg),
            (wu_hbm, wu), (cache_hbm, cache), (wo_hbm, wo), (wd_hbm, wd),
        )
    ):
        loads.append(pltpu.make_async_copy(src, dst, load_sems.at[i]))
        loads[-1].start()
    loads[0].wait()
    fold(hidden, every.at[me.z, me.x, me.y], stats)
    greet(me)

    first_axis = ("x", "y", "x", "y")
    last_axis = ("y", "x", "y", "x")

    def send_own(e):
        z = (me.z + e) % 4
        own = every.at[z, me.x, me.y]
        return [wire.send(own, own, me.at(**{first_axis[e]: d})) for d in (1, 2, 3)]

    def send_line(e):
        z = (me.z + e) % 4
        line = every.at[z, :, me.y] if first_axis[e] == "x" else every.at[z, me.x]
        return [wire.send(line, line, me.at(**{last_axis[e]: d})) for d in (1, 2, 3)]

    own = every.at[me.z, me.x, me.y]
    sums = [wire.send(stats.at[0], stats.at[d], me.at(zh=d // 2, c=d % 2)) for d in (1, 2, 3)]
    shards = [wire.send(own, own, me.at(z=d)) for d in (1, 2, 3)]
    owns = [send_own(0)]
    arrive(shards)
    owns += [send_own(e) for e in (1, 2, 3)]
    arrive(owns[0])
    lines = [send_line(0)]
    arrive(sums)
    known[me.x, me.z, me.y] = moments(stats)
    mine = known.at[me.x, me.z, me.y]
    facts = [wire.send(mine, mine, me.at(z=d)) for d in (1, 2, 3)]
    for e in (1, 2, 3):
        arrive(owns[e])
        lines.append(send_line(e))
    arrive(facts)
    mine = known.at[me.x, :, me.y]
    facts = [wire.send(mine, mine, me.at(x=d)) for d in (1, 2, 3)]
    write_picks(me, pick_in, pick_mid, pick_out)
    arrive(facts)
    mine = known.at[:, :, me.y]
    facts = [wire.send(mine, mine, me.at(y=d)) for d in (1, 2, 3)]
    for i in (1, 2, 3, 4):
        loads[i].wait()
    arrive(facts)

    far = 1 - me.zh
    near, across = [None, None], [None, None]

    def send_core(p):
        src = gu.at[pl.ds(2 * p, 2), :, 1 - me.c]
        near[p] = wire.send(src, gu_in.at[p], me.at(c=1))

    def send_far(p):
        arrive([near[p]])
        add_cores(me, p, far, gu, gu_in, gu_sum)
        across[p] = wire.send(gu_sum.at[p, far], gu_far.at[p], me.at(zh=1))
        add_cores(me, p, me.zh, gu, gu_in, gu_sum)

    def send_hidden(p):
        arrive([across[p]])
        activate(me, p, gu_sum, gu_far, blocks)
        own = blocks.at[pl.ds(2 * p, 2), me.zh, me.c]
        across[p] = wire.send(own, own, me.at(zh=1))

    def send_pair(p):
        arrive([across[p]])
        pair = blocks.at[pl.ds(2 * p, 2), :, me.c]
        near[p] = wire.send(pair, pair, me.at(c=1))

    arrive(lines[0] + lines[1])
    normalise(me, 0, every, known, gain, normed)
    gate_up_products(0, normed, wg, wu, gu)
    send_core(0)
    qkv_products(0, normed, wq, qkv)
    send_far(0)
    arrive(lines[2] + lines[3])
    normalise(me, 1, every, known, gain, normed)
    qkv_products(1, normed, wq, qkv)

    def qkv_piece(c, d):
        return qkv.at[(me.x + d - me.z + 4) % 4, :, (me.c + c) % 2]

    copies = two_way(me, wire, "x", "c", qkv_piece, s1)
    s1[0, me.x] = qkv[(me.x - me.z + 4) % 4, :, me.c]
    gate_up_products(1, normed, wg, wu, gu)
    send_core(1)
    arrive(copies)
    mixed = (s1[0].astype(F32) + s1[1].astype(F32)).reshape(4, 2, 4, 8, 128)
    for h in range(2):
        for t in range(4):
            q2[h, t] = mixed[:, h, t].reshape(32, 128).astype(BF16)
    copies = two_way(
        me, wire, "z", "zh", lambda h, d: q2.at[(me.zh + h) % 2, (me.z + d) % 4], s2
    )
    s2[0, me.z] = q2[me.zh, me.z]
    send_far(1)
    arrive(copies)
    s2_sum[...] = (s2[0].astype(F32) + s2[1].astype(F32)).astype(BF16)
    copies = [wire.send(s2_sum, s3.at[me.y], me.at(y=d)) for d in (1, 2, 3)]
    s3[me.y] = s2_sum[...]
    loads[5].wait()
    arrive(copies)
    g_ref[...] = dot(pick_in[...], s3[...].reshape(512, 128))
    attend(lengths_ref[0], g_ref, cache, t_ref, flat, heads32, fresh_v, flat_out, t_wide)

    copies = two_way(me, wire, "x", "c", lambda c, d: t_ref.at[(me.x + d) % 4], u1)
    u1[0, me.x] = t_ref[me.x]
    send_hidden(0)
    arrive(copies)
    mixed = u1[...].astype(F32).reshape(8, 4, 8, 128)
    for t in range(4):
        u1_sorted[t] = mixed[:, t].reshape(64, 128).astype(BF16)
    copies = two_way(me, wire, "z", "zh", lambda h, d: u1_sorted.at[(me.z + d) % 4], u2)
    u2[0, me.z] = u1_sorted[me.z]
    send_hidden(1)
    send_pair(0)
    arrive(copies)
    u2_sorted[...] = (
        dot(pick_mid[...], u2[...].reshape(512, 128)).astype(BF16).reshape(4, 128, 128)
    )
    copies = [
        wire.send(u2_sorted.at[(me.y + d) % 4], u3.at[me.y], me.at(y=d)) for d in (1, 2, 3)
    ]
    u3[me.y] = u2_sorted[me.y]
    for i in (6, 7):
        loads[i].wait()
    arrive(copies)
    heads[...] = dot(pick_out[...], u3[...].reshape(512, 128)).astype(BF16)

    def send_rows(e):
        copies = []
        for d in (1, 2, 3):
            if last_axis[e] == "y":
                src = partial.at[e, :, (me.y + d) % 4]
            else:
                src = partial.at[e, (me.x + d) % 4]
            copies.append(wire.send(src, ra.at[e, d - 1], me.at(**{last_axis[e]: d})))
        return copies

    def send_row(e, copies):
        arrive(copies)

        def body(i, _):
            if last_axis[e] == "y":
                total = partial[e, i, me.y].astype(F32)
            else:
                total = partial[e, me.x, i].astype(F32)
            for d in range(3):
                total = total + ra[e, d, i].astype(F32)
            sa[e, i] = total.astype(BF16)
            return 0

        lax.fori_loop(0, 4, body, 0)
        here = getattr(me, first_axis[e])
        return [
            wire.send(sa.at[e, (here + d) % 4], rb.at[e, d - 1], me.at(**{first_axis[e]: d}))
            for d in (1, 2, 3)
        ]

    def row_sum(e, copies):
        arrive(copies)
        total = sa[e, getattr(me, first_axis[e])].astype(F32)
        for d in range(3):
            total = total + rb[e, d].astype(F32)
        return total

    def send_block(e, copies):
        sz[e - 1] = row_sum(e, copies).astype(BF16)
        return wire.send(sz.at[e - 1], rz.at[e - 1], me.at(z=e))

    rows = {}
    arrive([near[0]])
    second_products(0, blocks, heads, wo, wd, partial)
    rows[1] = send_rows(1)
    rows[0] = send_rows(0)
    send_pair(1)
    arrive([near[1]])
    second_products(1, blocks, heads, wo, wd, partial)
    rows[2] = send_rows(2)
    rows[3] = send_rows(3)
    row = {1: send_row(1, rows[1])}
    row[0] = send_row(0, rows[0])
    row[2] = send_row(2, rows[2])
    ends = [send_block(1, row[1])]
    row[3] = send_row(3, rows[3])
    ends.append(send_block(2, row[2]))
    total = row_sum(0, row[0])
    ends.append(send_block(3, row[3]))
    arrive(ends)
    for e in range(3):
        total = total + rz[e].astype(F32)
    whole = jnp.concatenate([total[:8], total[8:]], 1)
    for step in range(STEPS):
        out_ref[step] = (
            hidden[step].astype(F32) + whole[4 * step : 4 * step + 4]
        ).astype(BF16)
    wire.close()


def per_device(hidden_in, norm_gain, w_qkv, w_gate, w_up, w_out, w_down, kv_cache, lengths):
    far = pl.BlockSpec(memory_space=pltpu.HBM)
    scratch = [
        ((2, 4, WIDTH), BF16), ((1, WIDTH), F32), ((QCOLS, WIDTH), BF16), ((UNITS, WIDTH), BF16),
        ((UNITS, WIDTH), BF16), ((OCOLS, WIDTH), BF16), ((UNITS, WIDTH), BF16),
        ((1, CTX, 512), BF16), 8,
        ((4, 2, 8, 128), F32), ((4, 4, 4, 8, 128), F32), ((4, 4, 4, 16, HALF), BF16),
        ((512, WIDTH), BF16), ((4, 2, 2, 32, 128), BF16), ((4, 2, 2, 32, HALF), BF16),
        ((2, 2, 2, 32, HALF), BF16), ((2, 2, 2, 32, HALF), BF16), ((2, 2, 32, HALF), BF16),
        ((4, 2, 2, 32, 640), BF16),
        ((2, 4, 2, 32, 128), BF16), ((2, 4, 32, 128), BF16), ((2, 4, 32, 128), BF16),
        ((4, 32, 128), BF16), ((4, 4, 32, 128), BF16), ((128, 128), F32), ((4, 32, 128), BF16),
        ((2, 6656), F32), ((56, 256), F32), ((16, 256), F32), ((2, 6144), F32), ((128, 128), F32),
        ((2, 4, 32, 128), BF16), ((4, 64, 128), BF16), ((2, 4, 64, 128), BF16),
        ((4, 128, 128), BF16), ((4, 128, 128), BF16), ((512, 128), BF16),
        ((128, 512), BF16), ((512, 512), BF16), ((512, 512), BF16),
        ((4, 4, 4, 16, HALF), BF16), ((4, 3, 4, 16, HALF), BF16), ((4, 4, 16, HALF), BF16),
        ((4, 3, 16, HALF), BF16), ((3, 16, HALF), BF16), ((3, 16, HALF), BF16),
        128, 128,
    ]
    return pl.pallas_call(
        kernel,
        name="layer",
        out_shape=jax.ShapeDtypeStruct((2, 4, WIDTH), BF16),
        in_specs=[pl.BlockSpec(memory_space=pltpu.SMEM)] + [far] * 8,
        out_specs=pl.BlockSpec(memory_space=pltpu.VMEM),
        scratch_shapes=[
            pltpu.SemaphoreType.DMA((entry,)) if isinstance(entry, int) else pltpu.VMEM(*entry)
            for entry in scratch
        ],
        compiler_params=pltpu.CompilerParams(
            collective_id=0, has_side_effects=True, vmem_limit_bytes=56 * 2**20
        ),
    )(
        lengths, hidden_in, norm_gain.reshape(1, WIDTH), w_qkv.T, w_gate.T, w_up.T,
        w_out, w_down, kv_cache,
    )


def solution(mesh):
    return jax.shard_map(
        per_device,
        mesh=mesh,
        in_specs=(
            P(None, "yz", "gx"),
            P("gx"),
            P("gx", "yz"),
            P("gx", "yz"),
            P("gx", "yz"),
            P("yz", "gx"),
            P("yz", "gx"),
            P(("gx", "yz"), None, None),
            P(("gx", "yz")),
        ),
        out_specs=P(None, "yz", "gx"),
        check_vma=False,
    )
```

```python
import jax
import jax.numpy as jnp
from jax import lax
from jax.experimental import pallas as pl
from jax.experimental.pallas import tpu as pltpu
from jax.sharding import PartitionSpec as P

D = 9216
HEADS = 24
HEAD_DIM = 256
CTX = 2048
STEPS = 2
EPS = 1e-06
SCALE = 0.0625
WIDTH = 2304
HALF = 1152
UNITS = 576
QCOLS = 104
OCOLS = 96
MESH = pl.DeviceIdType.MESH
F32 = jnp.float32
BF16 = jnp.bfloat16


class Place:
    def __init__(self):
        g = lax.axis_index("gx")
        j = lax.axis_index("yz")
        self.g, self.j = g, j
        self.zh, self.c = g // 2, g % 2
        self.x, self.z, self.y = j // 16, (j // 4) % 4, j % 4

    def at(self, zh=0, c=0, x=0, z=0, y=0):
        g = ((self.zh + zh) % 2) * 2 + (self.c + c) % 2
        j = ((self.x + x) % 4) * 16 + ((self.z + z) % 4) * 4 + (self.y + y) % 4
        return (g, j)


def greet(me):
    barrier = pltpu.get_barrier_semaphore()
    count = 0
    for d in (1, 2, 3):
        partners = [me.at(x=d), me.at(z=d), me.at(y=d), me.at(c=1, x=d), me.at(zh=1, z=d)]
        if d < 3:
            partners.append(me.at(zh=d // 2, c=d % 2))
        for target in partners:
            pl.semaphore_signal(barrier, inc=1, device_id=target, device_id_type=MESH)
            count += 1
    pl.semaphore_wait(barrier, count)


class Wire:
    def __init__(self, send_sems, recv_sems):
        self.send_sems, self.recv_sems = send_sems, recv_sems
        self.used = 0
        self.open = []

    def send(self, src, dst, target):
        copy = pltpu.make_async_remote_copy(
            src_ref=src,
            dst_ref=dst,
            send_sem=self.send_sems.at[self.used],
            recv_sem=self.recv_sems.at[self.used],
            device_id=target,
            device_id_type=MESH,
        )
        self.used += 1
        copy.start()
        self.open.append(copy)
        return copy

    def close(self):
        for copy in self.open:
            copy.wait_send()


def arrive(copies):
    for copy in copies:
        copy.wait_recv()


def dot(a, b):
    return jnp.dot(a, b, preferred_element_type=F32)


def dot_t(a, b):
    return lax.dot_general(a, b, (((1,), (1,)), ((), ())), preferred_element_type=F32)


def fold(hidden, own, part):
    rows = jnp.concatenate([hidden[0].astype(F32), hidden[1].astype(F32)], 0)
    own[...] = jnp.concatenate([rows[:, :HALF], rows[:, HALF:]], 0).astype(BF16)
    lane = lax.broadcasted_iota(jnp.int32, (8, 128), 1)
    sums = jnp.sum(rows, 1, keepdims=True)
    squares = jnp.sum(rows * rows, 1, keepdims=True)
    part[...] = jnp.where(lane < 64, sums, squares)


def normalise(me, raw, sums, gain, every):
    def body(z, _):
        total = (sums[0, z] + sums[1, z]) / D
        mean = total[:, :1]
        var = total[:, 64:65] - mean * mean
        scale = lax.rsqrt(var + EPS)
        block = raw[z].astype(F32)
        left = (block[:8] - mean) * scale * gain[:, :HALF]
        right = (block[8:] - mean) * scale * gain[:, HALF:]
        every[z, me.x, me.y] = jnp.concatenate([left, right], 0).astype(BF16)
        return 0

    lax.fori_loop(0, 4, body, 0)


def unfold(me, e, every, normed):
    z = (me.z + e) % 4

    def body(i, _):
        block = every[z, i].astype(F32)
        rows = pl.ds(pl.multiple_of(e * 128 + i * 32, 32), 32)
        normed[rows, :HALF] = block[:, :8].reshape(32, HALF).astype(BF16)
        normed[rows, HALF:] = block[:, 8:].reshape(32, HALF).astype(BF16)
        return 0

    lax.fori_loop(0, 4, body, 0)


def qkv_products(p, normed, wq, qkv):
    part = dot_t(normed[256 * p : 256 * p + 256, :], wq[...])
    part = jnp.concatenate([part, jnp.zeros((256, 24), F32)], 1)
    qkv[2 * p : 2 * p + 2] = part.reshape(2, 2, 2, 32, 128).astype(BF16)


def gate_up_products(p, normed, wg, wu, gu):
    rows = normed[256 * p : 256 * p + 256, :]
    gate = dot_t(rows, wg[...])
    up = dot_t(rows, wu[...])
    tail = jnp.concatenate([gate[:, 512:], up[:, 512:]], 1)
    own = slice(2 * p, 2 * p + 2)
    gu[own, :, :, :, :512] = gate[:, :512].reshape(2, 2, 2, 32, 512).astype(BF16)
    gu[own, :, :, :, 512:1024] = up[:, :512].reshape(2, 2, 2, 32, 512).astype(BF16)
    gu[own, :, :, :, 1024:] = tail.reshape(2, 2, 2, 32, 128).astype(BF16)


def add_cores(me, p, half, gu, gu_in, gu_sum):
    def body(e, _):
        total = gu[2 * p + e, half, me.c].astype(F32) + gu_in[p, e, half].astype(F32)
        gu_sum[p, half, e] = total.astype(BF16)
        return 0

    lax.fori_loop(0, 2, body, 0)


def activate(me, p, gu_sum, gu_far, blocks):
    def body(e, _):
        total = gu_sum[p, me.zh, e].astype(F32) + gu_far[p, e].astype(F32)
        gate, up = total[:, :512], total[:, 512:1024]
        tail = total[:, 1024:]
        last = tail / (1.0 + jnp.exp(-tail)) * pltpu.roll(tail, 64, 1)
        lane = lax.broadcasted_iota(jnp.int32, last.shape, 1)
        blocks[2 * p + e, me.zh, me.c, :, :512] = (gate / (1.0 + jnp.exp(-gate)) * up).astype(BF16)
        blocks[2 * p + e, me.zh, me.c, :, 512:] = jnp.where(lane < 64, last, 0.0).astype(BF16)
        return 0

    lax.fori_loop(0, 2, body, 0)


def two_way(me, wire, along, other, piece, landing):
    copies = []
    for b in (0, 1):
        for d in range(4):
            if b or d:
                target = me.at(**{other: b, along: d})
                copies.append(wire.send(piece(b, d), landing.at[b, getattr(me, along)], target))
    return copies


def attend(length, g_ref, cache, t_ref, flat, heads, fresh_v, flat_out, t_wide):
    for j in range(64):
        flat[:, QCOLS * j : QCOLS * j + QCOLS] = g_ref[2 * j : 2 * j + 2, :QCOLS]
    heads[48:56, :] = jnp.zeros((8, 256), F32)
    for h in range(HEADS + 1):
        heads[2 * h : 2 * h + 2, :] = flat[:, 256 * h : 256 * h + 256]
    lane = lax.broadcasted_iota(jnp.int32, (8, 128), 1).astype(F32)
    freqs = 10000.0 ** (-lane / 128.0)
    step8 = (lax.broadcasted_iota(jnp.int32, (8, 128), 0) & 1).astype(F32)
    angle = (length.astype(F32) + step8) * freqs
    cosine = jnp.concatenate([jnp.cos(angle)] * 7, 0)
    sine = jnp.concatenate([jnp.sin(angle)] * 7, 0)
    first, second = heads[:, :128], heads[:, 128:]
    turned = jnp.concatenate(
        [first * cosine - second * sine, second * cosine + first * sine], 1
    )
    queries = turned[: 2 * HEADS].astype(BF16)
    fresh = turned[2 * HEADS :]
    fresh_k = jnp.concatenate([fresh, jnp.zeros((8, 256), F32)], 0).astype(BF16)
    fresh_v[...] = jnp.zeros((16, 256), F32)
    fresh_v[0:2, :] = flat[:, 6400:6656]
    keys = cache[0, :, :256]
    values = cache[0, :, 256:]
    old = dot_t(queries, keys) * SCALE
    slot = lax.broadcasted_iota(jnp.int32, old.shape, 1)
    old = jnp.where(slot < length, old, -1e30)
    new = dot_t(queries, fresh_k) * SCALE
    new_slot = lax.broadcasted_iota(jnp.int32, new.shape, 1)
    new_step = lax.broadcasted_iota(jnp.int32, new.shape, 0) & 1
    new = jnp.where(new_slot <= new_step, new, -1e30)
    peak = jnp.maximum(jnp.max(old, 1, keepdims=True), jnp.max(new, 1, keepdims=True))
    old = jnp.exp(old - peak)
    new = jnp.exp(new - peak)
    total = jnp.sum(old, 1, keepdims=True) + jnp.sum(new, 1, keepdims=True)
    mixed = dot((old / total).astype(BF16), values) + dot(
        (new / total).astype(BF16), fresh_v[...].astype(BF16)
    )
    heads[: 2 * HEADS, :] = mixed
    for h in range(HEADS):
        flat_out[:, 256 * h : 256 * h + 256] = heads[2 * h : 2 * h + 2, :]
    t_wide[...] = jnp.zeros((128, 128), F32)
    for j in range(64):
        t_wide[2 * j : 2 * j + 2, :OCOLS] = flat_out[:, OCOLS * j : OCOLS * j + OCOLS]
    t_ref[...] = t_wide[...].astype(BF16).reshape(4, 32, 128)


def write_picks(me, pick_in, pick_mid, pick_out):
    def write(pick, wanted, keep):
        rows, depth = pick.shape
        row = lax.broadcasted_iota(jnp.int32, (64, depth), 0)
        col = lax.broadcasted_iota(jnp.int32, (64, depth), 1)
        place = jnp.where(keep(col), wanted(col), -1)

        def body(i, _):
            at = pl.ds(pl.multiple_of(i * 64, 64), 64)
            pick[at, :] = jnp.where(row + i * 64 == place, 1.0, 0.0).astype(BF16)
            return 0

        lax.fori_loop(0, rows // 64, body, 0)

    def bits(k, low, count):
        return (k >> low) & ((1 << count) - 1)

    def arrived(k):
        return bits(k, 3, 2) * 32 + bits(k, 5, 2) * 8 + bits(k, 7, 2) * 2 + bits(k, 2, 1)

    def sorted_by_y(k):
        return (
            bits(k, 1, 2) * 128 + bits(k, 8, 1) * 64 + bits(k, 5, 1) * 32
            + bits(k, 6, 2) * 8 + bits(k, 3, 2) * 2 + bits(k, 0, 1)
        )

    def by_row(k):
        chunk = (bits(k, 1, 2) - me.z) & 3
        block = ((bits(k, 6, 1) + me.zh) & 1) * 2 + ((bits(k, 5, 1) + me.c) & 1)
        return chunk * 128 + block * 32 + bits(k, 3, 2) * 8 + bits(k, 0, 1) * 4 + bits(k, 7, 2)

    write(pick_in, arrived, lambda k: bits(k, 0, 2) == me.y)
    write(pick_mid, sorted_by_y, lambda k: k >= 0)
    write(pick_out, by_row, lambda k: k >= 0)


def down_products(p, blocks, wd, early):
    lines = blocks[2 * p : 2 * p + 2].reshape(256, 640)
    for n in range(0, WIDTH, 384):
        columns = slice(n, n + 384)
        early[:, columns] = dot(lines[:, :512], wd[:512, columns]) + dot(
            lines[:, 512:UNITS], wd[512:, columns]
        )


def out_products(p, early, heads, wo, partial):
    attended = heads[256 * p : 256 * p + 256, :OCOLS]
    for n in range(0, HALF, 384):
        sides = []
        for at in (n, HALF + n):
            columns = slice(at, at + 384)
            product = early[:, columns] + dot(attended, wo[:, columns])
            sides.append(product.reshape(2, 4, 4, 8, 384))
        partial[2 * p : 2 * p + 2, :, :, :, n : n + 384] = jnp.concatenate(sides, 3).astype(BF16)


def kernel(
    lengths_ref, hidden_hbm, gain_hbm, wq_hbm, wg_hbm, wu_hbm, wo_hbm, wd_hbm, cache_hbm, out_ref,
    hidden, gain, wq, wg, wu, wo, wd, cache, load_sems,
    part, part_in, pair, sums, raw, every, normed, qkv, gu, gu_in, gu_sum, gu_far, blocks,
    s1, q2, s2, s2_sum, s3, g_ref, t_ref, flat, heads32, fresh_v, flat_out, t_wide,
    u1, u1_sorted, u2, u2_sorted, u3, heads, pick_in, pick_mid, pick_out,
    early, partial, ra, sa, rb, sz, rz,
    send_sems, recv_sems,
):
    me = Place()
    wire = Wire(send_sems, recv_sems)
    loads = []
    for i, (src, dst) in enumerate(
        (
            (hidden_hbm, hidden), (gain_hbm, gain.at[0]), (wq_hbm, wq), (wg_hbm, wg),
            (wu_hbm, wu), (cache_hbm, cache), (wo_hbm, wo), (wd_hbm, wd),
        )
    ):
        loads.append(pltpu.make_async_copy(src, dst, load_sems.at[i]))
        loads[-1].start()
    loads[0].wait()
    fold(hidden, raw.at[me.z], part)
    greet(me)

    first_axis = ("x", "y", "x", "y")
    last_axis = ("y", "x", "y", "x")

    def send_own(e):
        z = (me.z + e) % 4
        own = every.at[z, me.x, me.y]
        return [wire.send(own, own, me.at(**{first_axis[e]: d})) for d in (1, 2, 3)]

    def send_line(e):
        z = (me.z + e) % 4
        line = every.at[z, :, me.y] if first_axis[e] == "x" else every.at[z, me.x]
        return [wire.send(line, line, me.at(**{last_axis[e]: d})) for d in (1, 2, 3)]

    swap = wire.send(part, part_in, me.at(c=1))
    own = raw.at[me.z]
    shards = [wire.send(own, own, me.at(z=d)) for d in (1, 2, 3)]
    arrive([swap])
    pair[...] = part[...] + part_in[...]
    sums[0, me.z] = pair[...]
    facts = two_way(me, wire, "z", "zh", lambda h, d: pair, sums)
    write_picks(me, pick_in, pick_mid, pick_out)
    loads[1].wait()
    arrive(shards)
    arrive(facts)
    normalise(me, raw, sums, gain, every)
    owns, lines = [send_own(e) for e in range(4)], [None] * 4
    for e in (0, 1):
        arrive(owns[e])
        lines[e] = send_line(e)
    for i in (2, 3, 4):
        loads[i].wait()
    arrive(owns[2] + owns[3])
    for e in (0, 1):
        arrive(lines[e])
        lines[e + 2] = send_line(e + 2)
        unfold(me, e, every, normed)

    far = 1 - me.zh
    near, across = [None, None], [None, None]

    def send_core(p):
        src = gu.at[pl.ds(2 * p, 2), :, 1 - me.c]
        near[p] = wire.send(src, gu_in.at[p], me.at(c=1))

    def send_far(p):
        arrive([near[p]])
        add_cores(me, p, far, gu, gu_in, gu_sum)
        across[p] = wire.send(gu_sum.at[p, far], gu_far.at[p], me.at(zh=1))
        add_cores(me, p, me.zh, gu, gu_in, gu_sum)

    def send_hidden(p):
        arrive([across[p]])
        activate(me, p, gu_sum, gu_far, blocks)
        own = blocks.at[pl.ds(2 * p, 2), me.zh, me.c]
        across[p] = wire.send(own, own, me.at(zh=1))

    def send_pair(p):
        arrive([across[p]])
        pair = blocks.at[pl.ds(2 * p, 2), :, me.c]
        near[p] = wire.send(pair, pair, me.at(c=1))

    gate_up_products(0, normed, wg, wu, gu)
    send_core(0)
    qkv_products(0, normed, wq, qkv)
    send_far(0)
    for e in (2, 3):
        arrive(lines[e])
        unfold(me, e, every, normed)
    qkv_products(1, normed, wq, qkv)

    def qkv_piece(c, d):
        return qkv.at[(me.x + d - me.z + 4) % 4, :, (me.c + c) % 2]

    copies = two_way(me, wire, "x", "c", qkv_piece, s1)
    s1[0, me.x] = qkv[(me.x - me.z + 4) % 4, :, me.c]
    gate_up_products(1, normed, wg, wu, gu)
    send_core(1)
    arrive(copies)
    mixed = (s1[0].astype(F32) + s1[1].astype(F32)).reshape(4, 2, 4, 8, 128)
    for h in range(2):
        for t in range(4):
            q2[h, t] = mixed[:, h, t].reshape(32, 128).astype(BF16)
    copies = two_way(
        me, wire, "z", "zh", lambda h, d: q2.at[(me.zh + h) % 2, (me.z + d) % 4], s2
    )
    s2[0, me.z] = q2[me.zh, me.z]
    send_far(1)
    arrive(copies)
    s2_sum[...] = (s2[0].astype(F32) + s2[1].astype(F32)).astype(BF16)
    copies = [wire.send(s2_sum, s3.at[me.y], me.at(y=d)) for d in (1, 2, 3)]
    s3[me.y] = s2_sum[...]
    send_hidden(0)
    loads[5].wait()
    arrive(copies)
    g_ref[...] = dot(pick_in[...], s3[...].reshape(512, 128))
    attend(lengths_ref[0], g_ref, cache, t_ref, flat, heads32, fresh_v, flat_out, t_wide)

    copies = two_way(me, wire, "x", "c", lambda c, d: t_ref.at[(me.x + d) % 4], u1)
    u1[0, me.x] = t_ref[me.x]
    send_pair(0)
    arrive(copies)
    mixed = u1[...].astype(F32).reshape(8, 4, 8, 128)
    for t in range(4):
        u1_sorted[t] = mixed[:, t].reshape(64, 128).astype(BF16)
    copies = two_way(me, wire, "z", "zh", lambda h, d: u1_sorted.at[(me.z + d) % 4], u2)
    u2[0, me.z] = u1_sorted[me.z]
    send_hidden(1)
    arrive(copies)
    u2_sorted[...] = (
        dot(pick_mid[...], u2[...].reshape(512, 128)).astype(BF16).reshape(4, 128, 128)
    )
    copies = [
        wire.send(u2_sorted.at[(me.y + d) % 4], u3.at[me.y], me.at(y=d)) for d in (1, 2, 3)
    ]
    u3[me.y] = u2_sorted[me.y]
    for i in (6, 7):
        loads[i].wait()
    arrive([near[0]])
    down_products(0, blocks, wd, early)
    send_pair(1)
    arrive(copies)
    heads[...] = dot(pick_out[...], u3[...].reshape(512, 128)).astype(BF16)

    def send_rows(e):
        copies = []
        for d in (1, 2, 3):
            if last_axis[e] == "y":
                src = partial.at[e, :, (me.y + d) % 4]
            else:
                src = partial.at[e, (me.x + d) % 4]
            copies.append(wire.send(src, ra.at[e, d - 1], me.at(**{last_axis[e]: d})))
        return copies

    def send_row(e, copies):
        arrive(copies)

        def body(i, _):
            if last_axis[e] == "y":
                total = partial[e, i, me.y].astype(F32)
            else:
                total = partial[e, me.x, i].astype(F32)
            for d in range(3):
                total = total + ra[e, d, i].astype(F32)
            sa[e, i] = total.astype(BF16)
            return 0

        lax.fori_loop(0, 4, body, 0)
        here = getattr(me, first_axis[e])
        return [
            wire.send(sa.at[e, (here + d) % 4], rb.at[e, d - 1], me.at(**{first_axis[e]: d}))
            for d in (1, 2, 3)
        ]

    def row_sum(e, copies):
        arrive(copies)
        total = sa[e, getattr(me, first_axis[e])].astype(F32)
        for d in range(3):
            total = total + rb[e, d].astype(F32)
        return total

    def send_block(e, copies):
        sz[e - 1] = row_sum(e, copies).astype(BF16)
        return wire.send(sz.at[e - 1], rz.at[e - 1], me.at(z=e))

    rows = {}
    out_products(0, early, heads, wo, partial)
    rows[1] = send_rows(1)
    rows[0] = send_rows(0)
    arrive([near[1]])
    down_products(1, blocks, wd, early)
    out_products(1, early, heads, wo, partial)
    rows[2] = send_rows(2)
    rows[3] = send_rows(3)
    row = {1: send_row(1, rows[1])}
    row[0] = send_row(0, rows[0])
    row[2] = send_row(2, rows[2])
    ends = [send_block(1, row[1])]
    row[3] = send_row(3, rows[3])
    ends.append(send_block(2, row[2]))
    total = row_sum(0, row[0])
    ends.append(send_block(3, row[3]))
    arrive(ends)
    for e in range(3):
        total = total + rz[e].astype(F32)
    whole = jnp.concatenate([total[:8], total[8:]], 1)
    for step in range(STEPS):
        out_ref[step] = (
            hidden[step].astype(F32) + whole[4 * step : 4 * step + 4]
        ).astype(BF16)
    wire.close()


def per_device(hidden_in, norm_gain, w_qkv, w_gate, w_up, w_out, w_down, kv_cache, lengths):
    far = pl.BlockSpec(memory_space=pltpu.HBM)
    scratch = [
        ((2, 4, WIDTH), BF16), ((1, WIDTH), F32), ((QCOLS, WIDTH), BF16), ((UNITS, WIDTH), BF16),
        ((UNITS, WIDTH), BF16), ((OCOLS, WIDTH), BF16), ((UNITS, WIDTH), BF16),
        ((1, CTX, 512), BF16), 8,
        ((8, 128), F32), ((8, 128), F32), ((8, 128), F32), ((2, 4, 8, 128), F32),
        ((4, 16, HALF), BF16), ((4, 4, 4, 16, HALF), BF16),
        ((512, WIDTH), BF16), ((4, 2, 2, 32, 128), BF16), ((4, 2, 2, 32, HALF), BF16),
        ((2, 2, 2, 32, HALF), BF16), ((2, 2, 2, 32, HALF), BF16), ((2, 2, 32, HALF), BF16),
        ((4, 2, 2, 32, 640), BF16),
        ((2, 4, 2, 32, 128), BF16), ((2, 4, 32, 128), BF16), ((2, 4, 32, 128), BF16),
        ((4, 32, 128), BF16), ((4, 4, 32, 128), BF16), ((128, 128), F32), ((4, 32, 128), BF16),
        ((2, 6656), F32), ((56, 256), F32), ((16, 256), F32), ((2, 6144), F32), ((128, 128), F32),
        ((2, 4, 32, 128), BF16), ((4, 64, 128), BF16), ((2, 4, 64, 128), BF16),
        ((4, 128, 128), BF16), ((4, 128, 128), BF16), ((512, 128), BF16),
        ((128, 512), BF16), ((512, 512), BF16), ((512, 512), BF16),
        ((256, WIDTH), F32), ((4, 4, 4, 16, HALF), BF16), ((4, 3, 4, 16, HALF), BF16), ((4, 4, 16, HALF), BF16),
        ((4, 3, 16, HALF), BF16), ((3, 16, HALF), BF16), ((3, 16, HALF), BF16),
        128, 128,
    ]
    return pl.pallas_call(
        kernel,
        name="layer",
        out_shape=jax.ShapeDtypeStruct((2, 4, WIDTH), BF16),
        in_specs=[pl.BlockSpec(memory_space=pltpu.SMEM)] + [far] * 8,
        out_specs=pl.BlockSpec(memory_space=pltpu.VMEM),
        scratch_shapes=[
            pltpu.SemaphoreType.DMA((entry,)) if isinstance(entry, int) else pltpu.VMEM(*entry)
            for entry in scratch
        ],
        compiler_params=pltpu.CompilerParams(
            collective_id=0, has_side_effects=True, vmem_limit_bytes=56 * 2**20
        ),
    )(
        lengths, hidden_in, norm_gain, w_qkv.T, w_gate.T, w_up.T,
        w_out, w_down, kv_cache,
    )


def solution(mesh):
    return jax.shard_map(
        per_device,
        mesh=mesh,
        in_specs=(
            P(None, "yz", "gx"),
            P("gx"),
            P("gx", "yz"),
            P("gx", "yz"),
            P("gx", "yz"),
            P("yz", "gx"),
            P("yz", "gx"),
            P(("gx", "yz"), None, None),
            P(("gx", "yz")),
        ),
        out_specs=P(None, "yz", "gx"),
        check_vma=False,
    )
```

```python
import jax
import jax.numpy as jnp
from jax import lax
from jax.experimental import pallas as pl
from jax.experimental.pallas import tpu as pltpu
from jax.sharding import PartitionSpec as P

D = 9216
HEADS = 24
HEAD_DIM = 256
CTX = 2048
STEPS = 2
EPS = 1e-06
SCALE = 0.0625
WIDTH = 2304
HALF = 1152
UNITS = 576
QCOLS = 104
OCOLS = 96
MESH = pl.DeviceIdType.MESH
F32 = jnp.float32
BF16 = jnp.bfloat16


class Place:
    def __init__(self):
        g = lax.axis_index("gx")
        j = lax.axis_index("yz")
        self.g, self.j = g, j
        self.zh, self.c = g // 2, g % 2
        self.x, self.z, self.y = j // 16, (j // 4) % 4, j % 4

    def at(self, zh=0, c=0, x=0, z=0, y=0):
        g = ((self.zh + zh) % 2) * 2 + (self.c + c) % 2
        j = ((self.x + x) % 4) * 16 + ((self.z + z) % 4) * 4 + (self.y + y) % 4
        return (g, j)


def greet(me):
    barrier = pltpu.get_barrier_semaphore()
    count = 0
    for d in (1, 2, 3):
        partners = [me.at(x=d), me.at(z=d), me.at(y=d), me.at(c=1, x=d), me.at(zh=1, z=d)]
        if d < 3:
            partners.append(me.at(zh=d // 2, c=d % 2))
        for target in partners:
            pl.semaphore_signal(barrier, inc=1, device_id=target, device_id_type=MESH)
            count += 1
    return count


class Wire:
    def __init__(self, send_sems, recv_sems):
        self.send_sems, self.recv_sems = send_sems, recv_sems
        self.used = 0
        self.open = []

    def send(self, src, dst, target):
        copy = pltpu.make_async_remote_copy(
            src_ref=src,
            dst_ref=dst,
            send_sem=self.send_sems.at[self.used],
            recv_sem=self.recv_sems.at[self.used],
            device_id=target,
            device_id_type=MESH,
        )
        self.used += 1
        copy.start()
        self.open.append(copy)
        return copy

    def close(self):
        for copy in self.open:
            copy.wait_send()


def arrive(copies):
    for copy in copies:
        copy.wait_recv()


def dot(a, b):
    return jnp.dot(a, b, preferred_element_type=F32)


def dot_t(a, b):
    return lax.dot_general(a, b, (((1,), (1,)), ((), ())), preferred_element_type=F32)


def fold(hidden, own, part):
    rows = jnp.concatenate([hidden[0].astype(F32), hidden[1].astype(F32)], 0)
    own[...] = jnp.concatenate([rows[:, :HALF], rows[:, HALF:]], 0).astype(BF16)
    lane = lax.broadcasted_iota(jnp.int32, (8, 128), 1)
    sums = jnp.sum(rows, 1, keepdims=True)
    squares = jnp.sum(rows * rows, 1, keepdims=True)
    part[...] = jnp.where(lane < 64, sums, squares)


def normalise(me, raw, sums, gain, every):
    def body(z, _):
        total = (sums[0, z] + sums[1, z]) / D
        mean = total[:, :1]
        var = total[:, 64:65] - mean * mean
        scale = lax.rsqrt(var + EPS)
        block = raw[z].astype(F32)
        left = (block[:8] - mean) * scale * gain[:, :HALF]
        right = (block[8:] - mean) * scale * gain[:, HALF:]
        every[z, me.x, me.y] = jnp.concatenate([left, right], 0).astype(BF16)
        return 0

    lax.fori_loop(0, 4, body, 0)


def unfold(me, e, every, normed):
    z = (me.z + e) % 4

    def body(i, _):
        block = every[z, i].astype(F32)
        rows = pl.ds(pl.multiple_of(e * 128 + i * 32, 32), 32)
        normed[rows, :HALF] = block[:, :8].reshape(32, HALF).astype(BF16)
        normed[rows, HALF:] = block[:, 8:].reshape(32, HALF).astype(BF16)
        return 0

    lax.fori_loop(0, 4, body, 0)


def qkv_products(first, planes, normed, wq, qkv):
    rows = 128 * planes
    part = dot_t(normed[128 * first : 128 * first + rows, :], wq[...])
    part = jnp.concatenate([part, jnp.zeros((rows, 24), F32)], 1)
    qkv[first : first + planes] = part.reshape(planes, 2, 2, 32, 128).astype(BF16)


def gate_up_products(e, normed, wg, wu, gu):
    rows = normed[128 * e : 128 * e + 128, :]
    gate = dot_t(rows, wg[...])
    up = dot_t(rows, wu[...])
    tail = jnp.concatenate([gate[:, 512:], up[:, 512:]], 1)
    gu[e, :, :, :, :512] = gate[:, :512].reshape(2, 2, 32, 512).astype(BF16)
    gu[e, :, :, :, 512:1024] = up[:, :512].reshape(2, 2, 32, 512).astype(BF16)
    gu[e, :, :, :, 1024:] = tail.reshape(2, 2, 32, 128).astype(BF16)


def add_cores(me, e, half, gu, gu_in, gu_sum):
    total = gu[e, half, me.c].astype(F32) + gu_in[e, half].astype(F32)
    gu_sum[e, half] = total.astype(BF16)


def activate(me, p, gu_sum, gu_far, blocks):
    def body(i, _):
        e = 2 * p + i
        total = gu_sum[e, me.zh].astype(F32) + gu_far[e].astype(F32)
        gate, up = total[:, :512], total[:, 512:1024]
        tail = total[:, 1024:]
        last = tail / (1.0 + jnp.exp(-tail)) * pltpu.roll(tail, 64, 1)
        lane = lax.broadcasted_iota(jnp.int32, last.shape, 1)
        blocks[e, me.zh, me.c, :, :512] = (gate / (1.0 + jnp.exp(-gate)) * up).astype(BF16)
        blocks[e, me.zh, me.c, :, 512:] = jnp.where(lane < 64, last, 0.0).astype(BF16)
        return 0

    lax.fori_loop(0, 2, body, 0)


def two_way(me, wire, along, other, piece, landing):
    copies = []
    for b in (0, 1):
        for d in range(4):
            if b or d:
                target = me.at(**{other: b, along: d})
                copies.append(wire.send(piece(b, d), landing.at[b, getattr(me, along)], target))
    return copies


def attend(length, g_ref, cache, t_ref, flat, heads, fresh_v, flat_out, t_wide):
    for j in range(64):
        flat[:, QCOLS * j : QCOLS * j + QCOLS] = g_ref[2 * j : 2 * j + 2, :QCOLS]
    heads[48:56, :] = jnp.zeros((8, 256), F32)
    for h in range(HEADS + 1):
        heads[2 * h : 2 * h + 2, :] = flat[:, 256 * h : 256 * h + 256]
    lane = lax.broadcasted_iota(jnp.int32, (8, 128), 1).astype(F32)
    freqs = 10000.0 ** (-lane / 128.0)
    step8 = (lax.broadcasted_iota(jnp.int32, (8, 128), 0) & 1).astype(F32)
    angle = (length.astype(F32) + step8) * freqs
    cosine = jnp.concatenate([jnp.cos(angle)] * 7, 0)
    sine = jnp.concatenate([jnp.sin(angle)] * 7, 0)
    first, second = heads[:, :128], heads[:, 128:]
    turned = jnp.concatenate(
        [first * cosine - second * sine, second * cosine + first * sine], 1
    )
    queries = turned[: 2 * HEADS].astype(BF16)
    fresh = turned[2 * HEADS :]
    fresh_k = jnp.concatenate([fresh, jnp.zeros((8, 256), F32)], 0).astype(BF16)
    fresh_v[...] = jnp.zeros((16, 256), F32)
    fresh_v[0:2, :] = flat[:, 6400:6656]
    keys = cache[0, :, :256]
    values = cache[0, :, 256:]
    old = dot_t(queries, keys) * SCALE
    slot = lax.broadcasted_iota(jnp.int32, old.shape, 1)
    old = jnp.where(slot < length, old, -1e30)
    new = dot_t(queries, fresh_k) * SCALE
    new_slot = lax.broadcasted_iota(jnp.int32, new.shape, 1)
    new_step = lax.broadcasted_iota(jnp.int32, new.shape, 0) & 1
    new = jnp.where(new_slot <= new_step, new, -1e30)
    peak = jnp.maximum(jnp.max(old, 1, keepdims=True), jnp.max(new, 1, keepdims=True))
    old = jnp.exp(old - peak)
    new = jnp.exp(new - peak)
    total = jnp.sum(old, 1, keepdims=True) + jnp.sum(new, 1, keepdims=True)
    mixed = dot((old / total).astype(BF16), values) + dot(
        (new / total).astype(BF16), fresh_v[...].astype(BF16)
    )
    heads[: 2 * HEADS, :] = mixed
    for h in range(HEADS):
        flat_out[:, 256 * h : 256 * h + 256] = heads[2 * h : 2 * h + 2, :]
    t_wide[...] = jnp.zeros((128, 128), F32)
    for j in range(64):
        t_wide[2 * j : 2 * j + 2, :OCOLS] = flat_out[:, OCOLS * j : OCOLS * j + OCOLS]
    t_ref[...] = t_wide[...].astype(BF16).reshape(4, 32, 128)


def write_picks(me, pick_in, pick_mid, pick_out):
    def write(pick, wanted, keep):
        rows, depth = pick.shape
        row = lax.broadcasted_iota(jnp.int32, (64, depth), 0)
        col = lax.broadcasted_iota(jnp.int32, (64, depth), 1)
        place = jnp.where(keep(col), wanted(col), -1)

        def body(i, _):
            at = pl.ds(pl.multiple_of(i * 64, 64), 64)
            pick[at, :] = jnp.where(row + i * 64 == place, 1.0, 0.0).astype(BF16)
            return 0

        lax.fori_loop(0, rows // 64, body, 0)

    def bits(k, low, count):
        return (k >> low) & ((1 << count) - 1)

    def arrived(k):
        return bits(k, 3, 2) * 32 + bits(k, 5, 2) * 8 + bits(k, 7, 2) * 2 + bits(k, 2, 1)

    def sorted_by_y(k):
        return (
            bits(k, 1, 2) * 128 + bits(k, 8, 1) * 64 + bits(k, 5, 1) * 32
            + bits(k, 6, 2) * 8 + bits(k, 3, 2) * 2 + bits(k, 0, 1)
        )

    def by_row(k):
        chunk = (bits(k, 1, 2) - me.z) & 3
        block = ((bits(k, 6, 1) + me.zh) & 1) * 2 + ((bits(k, 5, 1) + me.c) & 1)
        return chunk * 128 + block * 32 + bits(k, 3, 2) * 8 + bits(k, 0, 1) * 4 + bits(k, 7, 2)

    write(pick_in, arrived, lambda k: bits(k, 0, 2) == me.y)
    write(pick_mid, sorted_by_y, lambda k: k >= 0)
    write(pick_out, by_row, lambda k: k >= 0)


def down_products(p, blocks, wd, early):
    lines = blocks[2 * p : 2 * p + 2].reshape(256, 640)
    for n in range(0, WIDTH, 384):
        columns = slice(n, n + 384)
        early[:, columns] = dot(lines[:, :512], wd[:512, columns]) + dot(
            lines[:, 512:UNITS], wd[512:, columns]
        )


def out_products(p, early, heads, wo, partial):
    attended = heads[256 * p : 256 * p + 256, :OCOLS]
    for n in range(0, HALF, 384):
        sides = []
        for at in (n, HALF + n):
            columns = slice(at, at + 384)
            product = early[:, columns] + dot(attended, wo[:, columns])
            sides.append(product.reshape(2, 4, 4, 8, 384))
        partial[2 * p : 2 * p + 2, :, :, :, n : n + 384] = jnp.concatenate(sides, 3).astype(BF16)


def kernel(
    lengths_ref, hidden_hbm, gain_hbm, wq_hbm, wg_hbm, wu_hbm, wo_hbm, wd_hbm, cache_hbm, out_ref,
    hidden, gain, wq, wg, wu, wo, wd, cache, load_sems,
    part, part_in, pair, sums, raw, every, normed, qkv, gu, gu_in, gu_sum, gu_far, blocks,
    s1, q2, s2, s2_sum, s3, g_ref, t_ref, flat, heads32, fresh_v, flat_out, t_wide,
    u1, u1_sorted, u2, u2_sorted, u3, heads, pick_in, pick_mid, pick_out,
    early, partial, ra, relay, sa, rb, sz, rz,
    send_sems, recv_sems,
):
    me = Place()
    wire = Wire(send_sems, recv_sems)
    loads = []
    for i, (src, dst) in enumerate(
        (
            (hidden_hbm, hidden), (gain_hbm, gain.at[0]), (wq_hbm, wq), (wg_hbm, wg),
            (wu_hbm, wu), (cache_hbm, cache), (wo_hbm, wo), (wd_hbm, wd),
        )
    ):
        loads.append(pltpu.make_async_copy(src, dst, load_sems.at[i]))
        loads[-1].start()
    count = greet(me)
    loads[0].wait()
    fold(hidden, raw.at[me.z], part)
    pl.semaphore_wait(pltpu.get_barrier_semaphore(), count)

    first_axis = ("x", "y", "x", "y")
    last_axis = ("y", "x", "y", "x")

    def send_own(e):
        z = (me.z + e) % 4
        own = every.at[z, me.x, me.y]
        return [wire.send(own, own, me.at(**{first_axis[e]: d})) for d in (1, 2, 3)]

    def send_line(e):
        z = (me.z + e) % 4
        line = every.at[z, :, me.y] if first_axis[e] == "x" else every.at[z, me.x]
        return [wire.send(line, line, me.at(**{last_axis[e]: d})) for d in (1, 2, 3)]

    swap = wire.send(part, part_in, me.at(c=1))
    own = raw.at[me.z]
    shards = [wire.send(own, own, me.at(z=d)) for d in (1, 2, 3)]
    arrive([swap])
    pair[...] = part[...] + part_in[...]
    sums[0, me.z] = pair[...]
    facts = two_way(me, wire, "z", "zh", lambda h, d: pair, sums)
    write_picks(me, pick_in, pick_mid, pick_out)
    loads[1].wait()
    arrive(shards)
    arrive(facts)
    normalise(me, raw, sums, gain, every)
    owns, lines = [send_own(e) for e in range(4)], [None] * 4
    for e in (0, 1):
        arrive(owns[e])
        lines[e] = send_line(e)
    for i in (2, 3, 4):
        loads[i].wait()
    arrive(owns[2] + owns[3])

    far = 1 - me.zh
    near, across = [None] * 4, [None] * 4

    def send_core(e):
        near[e] = wire.send(gu.at[e, :, 1 - me.c], gu_in.at[e], me.at(c=1))

    def send_far(e):
        arrive([near[e]])
        add_cores(me, e, far, gu, gu_in, gu_sum)
        across[e] = wire.send(gu_sum.at[e, far], gu_far.at[e], me.at(zh=1))
        add_cores(me, e, me.zh, gu, gu_in, gu_sum)

    def send_hidden(p):
        arrive(across[2 * p : 2 * p + 2])
        activate(me, p, gu_sum, gu_far, blocks)
        own = blocks.at[pl.ds(2 * p, 2), me.zh, me.c]
        across[p] = wire.send(own, own, me.at(zh=1))

    def send_pair(p):
        arrive([across[p]])
        pair = blocks.at[pl.ds(2 * p, 2), :, me.c]
        near[p] = wire.send(pair, pair, me.at(c=1))

    arrive(lines[0])
    lines[2] = send_line(2)
    unfold(me, 0, every, normed)
    gate_up_products(0, normed, wg, wu, gu)
    send_core(0)
    arrive(lines[1])
    lines[3] = send_line(3)
    unfold(me, 1, every, normed)
    send_far(0)
    gate_up_products(1, normed, wg, wu, gu)
    send_core(1)
    qkv_products(0, 2, normed, wq, qkv)
    send_far(1)
    arrive(lines[2])
    unfold(me, 2, every, normed)
    gate_up_products(2, normed, wg, wu, gu)
    send_core(2)
    qkv_products(2, 1, normed, wq, qkv)
    send_far(2)
    arrive(lines[3])
    unfold(me, 3, every, normed)
    qkv_products(3, 1, normed, wq, qkv)

    def qkv_piece(c, d):
        return qkv.at[(me.x + d - me.z + 4) % 4, :, (me.c + c) % 2]

    copies = two_way(me, wire, "x", "c", qkv_piece, s1)
    s1[0, me.x] = qkv[(me.x - me.z + 4) % 4, :, me.c]
    gate_up_products(3, normed, wg, wu, gu)
    send_core(3)
    arrive(copies)
    mixed = (s1[0].astype(F32) + s1[1].astype(F32)).reshape(4, 2, 4, 8, 128)
    for h in range(2):
        for t in range(4):
            q2[h, t] = mixed[:, h, t].reshape(32, 128).astype(BF16)
    copies = two_way(
        me, wire, "z", "zh", lambda h, d: q2.at[(me.zh + h) % 2, (me.z + d) % 4], s2
    )
    s2[0, me.z] = q2[me.zh, me.z]
    arrive(copies)
    s2_sum[...] = (s2[0].astype(F32) + s2[1].astype(F32)).astype(BF16)
    copies = [wire.send(s2_sum, s3.at[me.y], me.at(y=d)) for d in (1, 2, 3)]
    s3[me.y] = s2_sum[...]
    send_far(3)
    send_hidden(0)
    loads[5].wait()
    arrive(copies)
    g_ref[...] = dot(pick_in[...], s3[...].reshape(512, 128))
    attend(lengths_ref[0], g_ref, cache, t_ref, flat, heads32, fresh_v, flat_out, t_wide)

    copies = two_way(me, wire, "x", "c", lambda c, d: t_ref.at[(me.x + d) % 4], u1)
    u1[0, me.x] = t_ref[me.x]
    send_hidden(1)
    send_pair(0)
    arrive(copies)
    mixed = u1[...].astype(F32).reshape(8, 4, 8, 128)
    for t in range(4):
        u1_sorted[t] = mixed[:, t].reshape(64, 128).astype(BF16)
    copies = two_way(me, wire, "z", "zh", lambda h, d: u1_sorted.at[(me.z + d) % 4], u2)
    u2[0, me.z] = u1_sorted[me.z]
    arrive(copies)
    u2_sorted[...] = (
        dot(pick_mid[...], u2[...].reshape(512, 128)).astype(BF16).reshape(4, 128, 128)
    )
    copies = [
        wire.send(u2_sorted.at[(me.y + d) % 4], u3.at[me.y], me.at(y=d)) for d in (1, 2, 3)
    ]
    u3[me.y] = u2_sorted[me.y]
    for i in (6, 7):
        loads[i].wait()
    arrive([near[0]])
    down_products(0, blocks, wd, early)
    send_pair(1)
    arrive(copies)
    heads[...] = dot(pick_out[...], u3[...].reshape(512, 128)).astype(BF16)

    def half(e, t, h):
        if last_axis[e] == "y":
            return partial.at[e, pl.ds(2 * h, 2), t]
        return partial.at[e, t, pl.ds(2 * h, 2)]

    def ends_of(e):
        here = getattr(me, last_axis[e])
        return (
            [(here + d) % 4 for d in range(4)],
            me.at(**{last_axis[e]: 1}),
            me.at(**{last_axis[e]: 3}),
        )

    def send_rows(e):
        t, up, down = ends_of(e)
        relayed = [
            wire.send(half(e, t[2], 0), ra.at[e, 0], up),
            wire.send(half(e, t[2], 1), ra.at[e, 1], down),
        ]
        return relayed, [
            wire.send(half(e, t[1], 1), ra.at[e, 2], up),
            wire.send(half(e, t[3], 0), ra.at[e, 3], down),
        ]

    def relay_rows(e, relayed, direct):
        t, up, down = ends_of(e)
        arrive(relayed)
        relay[e, 0] = (half(e, t[1], 0)[...].astype(F32) + ra[e, 0].astype(F32)).astype(BF16)
        first = wire.send(relay.at[e, 0], ra.at[e, 4], up)
        relay[e, 1] = (half(e, t[3], 1)[...].astype(F32) + ra[e, 1].astype(F32)).astype(BF16)
        return direct + [first, wire.send(relay.at[e, 1], ra.at[e, 5], down)]

    def send_row(e, copies):
        arrive(copies)
        here = getattr(me, last_axis[e])
        for h, (a, b) in enumerate(((3, 4), (2, 5))):
            total = half(e, here, h)[...].astype(F32)
            total = total + ra[e, a].astype(F32) + ra[e, b].astype(F32)
            sa[e, 2 * h : 2 * h + 2] = total.astype(BF16)
        here = getattr(me, first_axis[e])
        return [
            wire.send(sa.at[e, (here + d) % 4], rb.at[e, d - 1], me.at(**{first_axis[e]: d}))
            for d in (1, 2, 3)
        ]

    def row_sum(e, copies):
        arrive(copies)
        total = sa[e, getattr(me, first_axis[e])].astype(F32)
        for d in range(3):
            total = total + rb[e, d].astype(F32)
        return total

    def send_block(e, copies):
        sz[e - 1] = row_sum(e, copies).astype(BF16)
        return wire.send(sz.at[e - 1], rz.at[e - 1], me.at(z=e))

    rows = {}
    out_products(0, early, heads, wo, partial)
    for e in (1, 0):
        rows[e] = send_rows(e)
    arrive([near[1]])
    down_products(1, blocks, wd, early)
    out_products(1, early, heads, wo, partial)
    for e in (2, 3):
        rows[e] = send_rows(e)
    for e in (1, 0, 2, 3):
        rows[e] = relay_rows(e, *rows[e])
    row = {1: send_row(1, rows[1])}
    row[0] = send_row(0, rows[0])
    row[2] = send_row(2, rows[2])
    ends = [send_block(1, row[1])]
    row[3] = send_row(3, rows[3])
    ends.append(send_block(2, row[2]))
    total = row_sum(0, row[0])
    ends.append(send_block(3, row[3]))
    arrive(ends)
    for e in range(3):
        total = total + rz[e].astype(F32)
    whole = jnp.concatenate([total[:8], total[8:]], 1)
    for step in range(STEPS):
        out_ref[step] = (
            hidden[step].astype(F32) + whole[4 * step : 4 * step + 4]
        ).astype(BF16)
    wire.close()


def per_device(hidden_in, norm_gain, w_qkv, w_gate, w_up, w_out, w_down, kv_cache, lengths):
    far = pl.BlockSpec(memory_space=pltpu.HBM)
    scratch = [
        ((2, 4, WIDTH), BF16), ((1, WIDTH), F32), ((QCOLS, WIDTH), BF16), ((UNITS, WIDTH), BF16),
        ((UNITS, WIDTH), BF16), ((OCOLS, WIDTH), BF16), ((UNITS, WIDTH), BF16),
        ((1, CTX, 512), BF16), 8,
        ((8, 128), F32), ((8, 128), F32), ((8, 128), F32), ((2, 4, 8, 128), F32),
        ((4, 16, HALF), BF16), ((4, 4, 4, 16, HALF), BF16),
        ((512, WIDTH), BF16), ((4, 2, 2, 32, 128), BF16), ((4, 2, 2, 32, HALF), BF16),
        ((4, 2, 32, HALF), BF16), ((4, 2, 32, HALF), BF16), ((4, 32, HALF), BF16),
        ((4, 2, 2, 32, 640), BF16),
        ((2, 4, 2, 32, 128), BF16), ((2, 4, 32, 128), BF16), ((2, 4, 32, 128), BF16),
        ((4, 32, 128), BF16), ((4, 4, 32, 128), BF16), ((128, 128), F32), ((4, 32, 128), BF16),
        ((2, 6656), F32), ((56, 256), F32), ((16, 256), F32), ((2, 6144), F32), ((128, 128), F32),
        ((2, 4, 32, 128), BF16), ((4, 64, 128), BF16), ((2, 4, 64, 128), BF16),
        ((4, 128, 128), BF16), ((4, 128, 128), BF16), ((512, 128), BF16),
        ((128, 512), BF16), ((512, 512), BF16), ((512, 512), BF16),
        ((256, WIDTH), F32), ((4, 4, 4, 16, HALF), BF16), ((4, 6, 2, 16, HALF), BF16),
        ((4, 2, 2, 16, HALF), BF16), ((4, 4, 16, HALF), BF16),
        ((4, 3, 16, HALF), BF16), ((3, 16, HALF), BF16), ((3, 16, HALF), BF16),
        128, 128,
    ]
    return pl.pallas_call(
        kernel,
        name="layer",
        out_shape=jax.ShapeDtypeStruct((2, 4, WIDTH), BF16),
        in_specs=[pl.BlockSpec(memory_space=pltpu.SMEM)] + [far] * 8,
        out_specs=pl.BlockSpec(memory_space=pltpu.VMEM),
        scratch_shapes=[
            pltpu.SemaphoreType.DMA((entry,)) if isinstance(entry, int) else pltpu.VMEM(*entry)
            for entry in scratch
        ],
        compiler_params=pltpu.CompilerParams(
            collective_id=0, has_side_effects=True, vmem_limit_bytes=56 * 2**20 - 160 * 2**10
        ),
    )(
        lengths, hidden_in, norm_gain, w_qkv.T, w_gate.T, w_up.T,
        w_out, w_down, kv_cache,
    )


def solution(mesh):
    return jax.shard_map(
        per_device,
        mesh=mesh,
        in_specs=(
            P(None, "yz", "gx"),
            P("gx"),
            P("gx", "yz"),
            P("gx", "yz"),
            P("gx", "yz"),
            P("yz", "gx"),
            P("yz", "gx"),
            P(("gx", "yz"), None, None),
            P(("gx", "yz")),
        ),
        out_specs=P(None, "yz", "gx"),
        check_vma=False,
    )
```

```python
import jax
import jax.numpy as jnp
from jax import lax
from jax.experimental import pallas as pl
from jax.experimental.pallas import tpu as pltpu
from jax.sharding import PartitionSpec as P

D = 9216
HEADS = 24
HEAD_DIM = 256
CTX = 2048
STEPS = 2
EPS = 1e-06
SCALE = 0.0625
WIDTH = 2304
HALF = 1152
UNITS = 576
QCOLS = 104
OCOLS = 96
MESH = pl.DeviceIdType.MESH
F32 = jnp.float32
BF16 = jnp.bfloat16


class Place:
    def __init__(self):
        g = lax.axis_index("gx")
        j = lax.axis_index("yz")
        self.g, self.j = g, j
        self.zh, self.c = g // 2, g % 2
        self.x, self.z, self.y = j // 16, (j // 4) % 4, j % 4

    def at(self, zh=0, c=0, x=0, z=0, y=0):
        g = ((self.zh + zh) % 2) * 2 + (self.c + c) % 2
        j = ((self.x + x) % 4) * 16 + ((self.z + z) % 4) * 4 + (self.y + y) % 4
        return (g, j)


def greet(me):
    barrier = pltpu.get_barrier_semaphore()
    count = 0
    for d in (1, 2, 3):
        partners = [me.at(x=d), me.at(z=d), me.at(y=d), me.at(c=1, x=d), me.at(zh=1, z=d)]
        if d < 3:
            partners.append(me.at(zh=d // 2, c=d % 2))
        for target in partners:
            pl.semaphore_signal(barrier, inc=1, device_id=target, device_id_type=MESH)
            count += 1
    return count


class Wire:
    def __init__(self, send_sems, recv_sems):
        self.send_sems, self.recv_sems = send_sems, recv_sems
        self.used = 0
        self.open = []

    def send(self, src, dst, target):
        copy = pltpu.make_async_remote_copy(
            src_ref=src,
            dst_ref=dst,
            send_sem=self.send_sems.at[self.used],
            recv_sem=self.recv_sems.at[self.used],
            device_id=target,
            device_id_type=MESH,
        )
        self.used += 1
        copy.start()
        self.open.append(copy)
        return copy

    def close(self):
        for copy in self.open:
            copy.wait_send()


def arrive(copies):
    for copy in copies:
        copy.wait_recv()


def dot(a, b):
    return jnp.dot(a, b, preferred_element_type=F32)


def dot_t(a, b):
    return lax.dot_general(a, b, (((1,), (1,)), ((), ())), preferred_element_type=F32)


def fold(hidden, own, part):
    rows = jnp.concatenate([hidden[0].astype(F32), hidden[1].astype(F32)], 0)
    own[...] = jnp.concatenate([rows[:, :HALF], rows[:, HALF:]], 0).astype(BF16)
    lane = lax.broadcasted_iota(jnp.int32, (8, 128), 1)
    sums = jnp.sum(rows, 1, keepdims=True)
    squares = jnp.sum(rows * rows, 1, keepdims=True)
    part[...] = jnp.where(lane < 64, sums, squares)


def normalise(me, raw, sums, gain, every):
    def body(z, _):
        total = (sums[0, z] + sums[1, z]) / D
        mean = total[:, :1]
        var = total[:, 64:65] - mean * mean
        scale = lax.rsqrt(var + EPS)
        block = raw[z].astype(F32)
        left = (block[:8] - mean) * scale * gain[:, :HALF]
        right = (block[8:] - mean) * scale * gain[:, HALF:]
        every[z, me.x, me.y] = jnp.concatenate([left, right], 0).astype(BF16)
        return 0

    lax.fori_loop(0, 4, body, 0)


def unfold(me, e, every, normed):
    z = (me.z + e) % 4

    def body(i, _):
        block = every[z, i].astype(F32)
        rows = pl.ds(pl.multiple_of(e * 128 + i * 32, 32), 32)
        normed[rows, :HALF] = block[:, :8].reshape(32, HALF).astype(BF16)
        normed[rows, HALF:] = block[:, 8:].reshape(32, HALF).astype(BF16)
        return 0

    lax.fori_loop(0, 4, body, 0)


def qkv_products(first, planes, normed, wq, qkv):
    rows = 128 * planes
    part = dot_t(normed[128 * first : 128 * first + rows, :], wq[...])
    part = jnp.concatenate([part, jnp.zeros((rows, 24), F32)], 1)
    qkv[first : first + planes] = part.reshape(planes, 2, 2, 32, 128).astype(BF16)


def gate_up_products(e, normed, wg, wu, gu):
    rows = normed[128 * e : 128 * e + 128, :]
    gate = dot_t(rows, wg[...])
    up = dot_t(rows, wu[...])
    tail = jnp.concatenate([gate[:, 512:], up[:, 512:]], 1)
    gu[e, :, :, :, :512] = gate[:, :512].reshape(2, 2, 32, 512).astype(BF16)
    gu[e, :, :, :, 512:1024] = up[:, :512].reshape(2, 2, 32, 512).astype(BF16)
    gu[e, :, :, :, 1024:] = tail.reshape(2, 2, 32, 128).astype(BF16)


def add_cores(me, e, half, gu, gu_in, gu_sum):
    total = gu[e, half, me.c].astype(F32) + gu_in[e, half].astype(F32)
    gu_sum[e, half] = total.astype(BF16)


def activate(me, p, gu_sum, gu_far, blocks):
    def body(i, _):
        e = 2 * p + i
        total = gu_sum[e, me.zh].astype(F32) + gu_far[e].astype(F32)
        gate, up = total[:, :512], total[:, 512:1024]
        tail = total[:, 1024:]
        last = tail / (1.0 + jnp.exp(-tail)) * pltpu.roll(tail, 64, 1)
        lane = lax.broadcasted_iota(jnp.int32, last.shape, 1)
        blocks[e, me.zh, me.c, :, :512] = (gate / (1.0 + jnp.exp(-gate)) * up).astype(BF16)
        blocks[e, me.zh, me.c, :, 512:] = jnp.where(lane < 64, last, 0.0).astype(BF16)
        return 0

    lax.fori_loop(0, 2, body, 0)


def two_way(me, wire, along, other, piece, landing):
    copies = []
    for b in (0, 1):
        for d in range(4):
            if b or d:
                target = me.at(**{other: b, along: d})
                copies.append(wire.send(piece(b, d), landing.at[b, getattr(me, along)], target))
    return copies


def attend(length, g_ref, cache, t_ref, flat, heads, fresh_v, flat_out, t_wide):
    for j in range(64):
        flat[:, QCOLS * j : QCOLS * j + QCOLS] = g_ref[2 * j : 2 * j + 2, :QCOLS]
    heads[48:56, :] = jnp.zeros((8, 256), F32)
    for h in range(HEADS + 1):
        heads[2 * h : 2 * h + 2, :] = flat[:, 256 * h : 256 * h + 256]
    lane = lax.broadcasted_iota(jnp.int32, (8, 128), 1).astype(F32)
    freqs = 10000.0 ** (-lane / 128.0)
    step8 = (lax.broadcasted_iota(jnp.int32, (8, 128), 0) & 1).astype(F32)
    angle = (length.astype(F32) + step8) * freqs
    cosine = jnp.concatenate([jnp.cos(angle)] * 7, 0)
    sine = jnp.concatenate([jnp.sin(angle)] * 7, 0)
    first, second = heads[:, :128], heads[:, 128:]
    turned = jnp.concatenate(
        [first * cosine - second * sine, second * cosine + first * sine], 1
    )
    queries = turned[: 2 * HEADS].astype(BF16)
    fresh = turned[2 * HEADS :]
    fresh_k = jnp.concatenate([fresh, jnp.zeros((8, 256), F32)], 0).astype(BF16)
    fresh_v[...] = jnp.zeros((16, 256), F32)
    fresh_v[0:2, :] = flat[:, 6400:6656]
    keys = cache[0, :, :256]
    values = cache[0, :, 256:]
    old = dot_t(queries, keys) * SCALE
    slot = lax.broadcasted_iota(jnp.int32, old.shape, 1)
    old = jnp.where(slot < length, old, -1e30)
    new = dot_t(queries, fresh_k) * SCALE
    new_slot = lax.broadcasted_iota(jnp.int32, new.shape, 1)
    new_step = lax.broadcasted_iota(jnp.int32, new.shape, 0) & 1
    new = jnp.where(new_slot <= new_step, new, -1e30)
    peak = jnp.maximum(jnp.max(old, 1, keepdims=True), jnp.max(new, 1, keepdims=True))
    old = jnp.exp(old - peak)
    new = jnp.exp(new - peak)
    total = jnp.sum(old, 1, keepdims=True) + jnp.sum(new, 1, keepdims=True)
    mixed = dot((old / total).astype(BF16), values) + dot(
        (new / total).astype(BF16), fresh_v[...].astype(BF16)
    )
    heads[: 2 * HEADS, :] = mixed
    for h in range(HEADS):
        flat_out[:, 256 * h : 256 * h + 256] = heads[2 * h : 2 * h + 2, :]
    t_wide[...] = jnp.zeros((128, 128), F32)
    for j in range(64):
        t_wide[2 * j : 2 * j + 2, :OCOLS] = flat_out[:, OCOLS * j : OCOLS * j + OCOLS]
    t_ref[...] = t_wide[...].astype(BF16).reshape(4, 32, 128)


def write_picks(me, pick_in, pick_mid, pick_out):
    def write(pick, wanted, keep):
        rows, depth = pick.shape
        row = lax.broadcasted_iota(jnp.int32, (64, depth), 0)
        col = lax.broadcasted_iota(jnp.int32, (64, depth), 1)
        place = jnp.where(keep(col), wanted(col), -1)

        def body(i, _):
            at = pl.ds(pl.multiple_of(i * 64, 64), 64)
            pick[at, :] = jnp.where(row + i * 64 == place, 1.0, 0.0).astype(BF16)
            return 0

        lax.fori_loop(0, rows // 64, body, 0)

    def bits(k, low, count):
        return (k >> low) & ((1 << count) - 1)

    def arrived(k):
        return bits(k, 3, 2) * 32 + bits(k, 5, 2) * 8 + bits(k, 7, 2) * 2 + bits(k, 2, 1)

    def sorted_by_y(k):
        return (
            bits(k, 1, 2) * 128 + bits(k, 8, 1) * 64 + bits(k, 5, 1) * 32
            + bits(k, 6, 2) * 8 + bits(k, 3, 2) * 2 + bits(k, 0, 1)
        )

    def by_row(k):
        chunk = (bits(k, 1, 2) - me.z) & 3
        block = ((bits(k, 6, 1) + me.zh) & 1) * 2 + ((bits(k, 5, 1) + me.c) & 1)
        return chunk * 128 + block * 32 + bits(k, 3, 2) * 8 + bits(k, 0, 1) * 4 + bits(k, 7, 2)

    write(pick_in, arrived, lambda k: bits(k, 0, 2) == me.y)
    write(pick_mid, sorted_by_y, lambda k: k >= 0)
    write(pick_out, by_row, lambda k: k >= 0)


def down_products(p, blocks, wd, early):
    lines = blocks[2 * p : 2 * p + 2].reshape(256, 640)
    for n in range(0, WIDTH, 384):
        columns = slice(n, n + 384)
        early[:, columns] = dot(lines[:, :512], wd[:512, columns]) + dot(
            lines[:, 512:UNITS], wd[512:, columns]
        )


def out_products(p, early, heads, wo, partial):
    attended = heads[256 * p : 256 * p + 256, :OCOLS]
    for n in range(0, HALF, 384):
        sides = []
        for at in (n, HALF + n):
            columns = slice(at, at + 384)
            product = early[:, columns] + dot(attended, wo[:, columns])
            sides.append(product.reshape(2, 4, 4, 8, 384))
        partial[2 * p : 2 * p + 2, :, :, :, n : n + 384] = jnp.concatenate(sides, 3).astype(BF16)


def kernel(
    lengths_ref, hidden_hbm, gain_hbm, wq_hbm, wg_hbm, wu_hbm, wo_hbm, wd_hbm, cache_hbm, out_ref,
    hidden, gain, wq, wg, wu, wo, wd, cache, load_sems,
    part, part_in, pair, sums, raw, every, normed, qkv, gu, gu_in, gu_sum, gu_far, blocks,
    s1, q2, s2, s2_sum, s3, g_ref, t_ref, flat, heads32, fresh_v, flat_out, t_wide,
    u1, u1_sorted, u2, u2_sorted, u3, heads, pick_in, pick_mid, pick_out,
    early, partial, ra, relay, sa, rb, sz, rz,
    send_sems, recv_sems,
):
    me = Place()
    wire = Wire(send_sems, recv_sems)
    loads = []
    for i, (src, dst) in enumerate(
        (
            (hidden_hbm, hidden), (gain_hbm, gain.at[0]), (wq_hbm, wq), (wg_hbm, wg),
            (wu_hbm, wu), (cache_hbm, cache), (wo_hbm, wo), (wd_hbm, wd),
        )
    ):
        loads.append(pltpu.make_async_copy(src, dst, load_sems.at[i]))
        loads[-1].start()
    count = greet(me)
    loads[0].wait()
    fold(hidden, raw.at[me.z], part)
    pl.semaphore_wait(pltpu.get_barrier_semaphore(), count)

    first_axis = ("x", "y", "x", "y")
    last_axis = ("y", "x", "y", "x")

    def send_own(e):
        z = (me.z + e) % 4
        own = every.at[z, me.x, me.y]
        return [wire.send(own, own, me.at(**{first_axis[e]: d})) for d in (1, 2, 3)]

    def send_line(e):
        z = (me.z + e) % 4
        line = every.at[z, :, me.y] if first_axis[e] == "x" else every.at[z, me.x]
        return [wire.send(line, line, me.at(**{last_axis[e]: d})) for d in (1, 2, 3)]

    swap = wire.send(part, part_in, me.at(c=1))
    own = raw.at[me.z]
    shards = [wire.send(own, own, me.at(z=d)) for d in (1, 2, 3)]
    arrive([swap])
    pair[...] = part[...] + part_in[...]
    sums[0, me.z] = pair[...]
    facts = two_way(me, wire, "z", "zh", lambda h, d: pair, sums)
    write_picks(me, pick_in, pick_mid, pick_out)
    loads[1].wait()
    arrive(shards)
    arrive(facts)
    normalise(me, raw, sums, gain, every)
    owns, lines = [send_own(e) for e in range(4)], [None] * 4
    for e in (0, 1):
        arrive(owns[e])
        lines[e] = send_line(e)
    for i in (2, 3, 4):
        loads[i].wait()
    arrive(owns[2] + owns[3])

    far = 1 - me.zh
    near, across = [None] * 4, [None] * 4

    def send_core(e):
        near[e] = wire.send(gu.at[e, :, 1 - me.c], gu_in.at[e], me.at(c=1))

    def send_far(e):
        arrive([near[e]])
        add_cores(me, e, far, gu, gu_in, gu_sum)
        across[e] = wire.send(gu_sum.at[e, far], gu_far.at[e], me.at(zh=1))
        add_cores(me, e, me.zh, gu, gu_in, gu_sum)

    def send_hidden(p):
        arrive(across[2 * p : 2 * p + 2])
        activate(me, p, gu_sum, gu_far, blocks)
        own = blocks.at[pl.ds(2 * p, 2), me.zh, me.c]
        across[p] = wire.send(own, own, me.at(zh=1))

    def send_pair(p):
        arrive([across[p]])
        pair = blocks.at[pl.ds(2 * p, 2), :, me.c]
        near[p] = wire.send(pair, pair, me.at(c=1))

    arrive(lines[0])
    lines[2] = send_line(2)
    unfold(me, 0, every, normed)
    gate_up_products(0, normed, wg, wu, gu)
    send_core(0)
    arrive(lines[1])
    lines[3] = send_line(3)
    unfold(me, 1, every, normed)
    send_far(0)
    gate_up_products(1, normed, wg, wu, gu)
    send_core(1)
    qkv_products(0, 2, normed, wq, qkv)
    send_far(1)
    arrive(lines[2])
    unfold(me, 2, every, normed)
    gate_up_products(2, normed, wg, wu, gu)
    send_core(2)
    qkv_products(2, 1, normed, wq, qkv)
    send_far(2)
    arrive(lines[3])
    unfold(me, 3, every, normed)
    qkv_products(3, 1, normed, wq, qkv)

    def qkv_piece(c, d):
        return qkv.at[(me.x + d - me.z + 4) % 4, :, (me.c + c) % 2]

    copies = two_way(me, wire, "x", "c", qkv_piece, s1)
    s1[0, me.x] = qkv[(me.x - me.z + 4) % 4, :, me.c]
    gate_up_products(3, normed, wg, wu, gu)
    send_core(3)
    arrive(copies)
    mixed = (s1[0].astype(F32) + s1[1].astype(F32)).reshape(4, 2, 4, 8, 128)
    for h in range(2):
        for t in range(4):
            q2[h, t] = mixed[:, h, t].reshape(32, 128).astype(BF16)
    copies = two_way(
        me, wire, "z", "zh", lambda h, d: q2.at[(me.zh + h) % 2, (me.z + d) % 4], s2
    )
    s2[0, me.z] = q2[me.zh, me.z]
    arrive(copies)
    s2_sum[...] = (s2[0].astype(F32) + s2[1].astype(F32)).astype(BF16)
    copies = [wire.send(s2_sum, s3.at[me.y], me.at(y=d)) for d in (1, 2, 3)]
    s3[me.y] = s2_sum[...]
    send_far(3)
    send_hidden(0)
    loads[5].wait()
    arrive(copies)
    g_ref[...] = dot(pick_in[...], s3[...].reshape(512, 128))
    attend(lengths_ref[0], g_ref, cache, t_ref, flat, heads32, fresh_v, flat_out, t_wide)

    copies = two_way(me, wire, "x", "c", lambda c, d: t_ref.at[(me.x + d) % 4], u1)
    u1[0, me.x] = t_ref[me.x]
    send_hidden(1)
    send_pair(0)
    arrive(copies)
    mixed = u1[...].astype(F32).reshape(8, 4, 8, 128)
    for t in range(4):
        u1_sorted[t] = mixed[:, t].reshape(64, 128).astype(BF16)
    copies = two_way(me, wire, "z", "zh", lambda h, d: u1_sorted.at[(me.z + d) % 4], u2)
    u2[0, me.z] = u1_sorted[me.z]
    arrive(copies)
    u2_sorted[...] = (
        dot(pick_mid[...], u2[...].reshape(512, 128)).astype(BF16).reshape(4, 128, 128)
    )
    copies = [
        wire.send(u2_sorted.at[(me.y + d) % 4], u3.at[me.y], me.at(y=d)) for d in (1, 2, 3)
    ]
    u3[me.y] = u2_sorted[me.y]
    for i in (6, 7):
        loads[i].wait()
    arrive([near[0]])
    down_products(0, blocks, wd, early)
    send_pair(1)
    arrive(copies)
    heads[...] = dot(pick_out[...], u3[...].reshape(512, 128)).astype(BF16)

    def half(e, t, h):
        if last_axis[e] == "y":
            return partial.at[e, pl.ds(2 * h, 2), t]
        return partial.at[e, t, pl.ds(2 * h, 2)]

    def ends_of(e):
        here = getattr(me, last_axis[e])
        return (
            [(here + d) % 4 for d in range(4)],
            me.at(**{last_axis[e]: 1}),
            me.at(**{last_axis[e]: 3}),
        )

    def send_rows(e):
        t, up, down = ends_of(e)
        relayed = [
            wire.send(half(e, t[2], 0), ra.at[e, 0], up),
            wire.send(half(e, t[2], 1), ra.at[e, 1], down),
        ]
        return relayed, [
            wire.send(half(e, t[1], 1), ra.at[e, 2], up),
            wire.send(half(e, t[3], 0), ra.at[e, 3], down),
        ]

    def relay_rows(e, relayed, direct):
        t, up, down = ends_of(e)
        arrive(relayed)
        relay[e, 0] = (half(e, t[1], 0)[...].astype(F32) + ra[e, 0].astype(F32)).astype(BF16)
        first = wire.send(relay.at[e, 0], ra.at[e, 4], up)
        relay[e, 1] = (half(e, t[3], 1)[...].astype(F32) + ra[e, 1].astype(F32)).astype(BF16)
        return direct + [first, wire.send(relay.at[e, 1], ra.at[e, 5], down)]

    def send_row(e, copies):
        arrive(copies)
        here = getattr(me, last_axis[e])
        for h, (a, b) in enumerate(((3, 4), (2, 5))):
            total = half(e, here, h)[...].astype(F32)
            total = total + ra[e, a].astype(F32) + ra[e, b].astype(F32)
            sa[e, 2 * h : 2 * h + 2] = total.astype(BF16)
        here = getattr(me, first_axis[e])
        return [
            wire.send(sa.at[e, (here + d) % 4], rb.at[e, d - 1], me.at(**{first_axis[e]: d}))
            for d in (1, 2, 3)
        ]

    def row_sum(e, copies):
        arrive(copies)
        total = sa[e, getattr(me, first_axis[e])].astype(F32)
        for d in range(3):
            total = total + rb[e, d].astype(F32)
        return total

    def send_block(e, copies):
        sz[e - 1] = row_sum(e, copies).astype(BF16)
        return wire.send(sz.at[e - 1], rz.at[e - 1], me.at(z=e))

    rows = {}
    out_products(0, early, heads, wo, partial)
    for e in (1, 0):
        rows[e] = send_rows(e)
    arrive([near[1]])
    down_products(1, blocks, wd, early)
    out_products(1, early, heads, wo, partial)
    for e in (2, 3):
        rows[e] = send_rows(e)
    for e in (1, 2, 3, 0):
        rows[e] = relay_rows(e, *rows[e])
    row = {1: send_row(1, rows[1])}
    row[2] = send_row(2, rows[2])
    ends = [send_block(1, row[1])]
    row[3] = send_row(3, rows[3])
    row[0] = send_row(0, rows[0])
    ends.append(send_block(2, row[2]))
    ends.append(send_block(3, row[3]))
    total = row_sum(0, row[0])
    arrive(ends)
    for e in range(3):
        total = total + rz[e].astype(F32)
    whole = jnp.concatenate([total[:8], total[8:]], 1)
    for step in range(STEPS):
        out_ref[step] = (
            hidden[step].astype(F32) + whole[4 * step : 4 * step + 4]
        ).astype(BF16)
    wire.close()


def per_device(hidden_in, norm_gain, w_qkv, w_gate, w_up, w_out, w_down, kv_cache, lengths):
    far = pl.BlockSpec(memory_space=pltpu.HBM)
    scratch = [
        ((2, 4, WIDTH), BF16), ((1, WIDTH), F32), ((QCOLS, WIDTH), BF16), ((UNITS, WIDTH), BF16),
        ((UNITS, WIDTH), BF16), ((OCOLS, WIDTH), BF16), ((UNITS, WIDTH), BF16),
        ((1, CTX, 512), BF16), 8,
        ((8, 128), F32), ((8, 128), F32), ((8, 128), F32), ((2, 4, 8, 128), F32),
        ((4, 16, HALF), BF16), ((4, 4, 4, 16, HALF), BF16),
        ((512, WIDTH), BF16), ((4, 2, 2, 32, 128), BF16), ((4, 2, 2, 32, HALF), BF16),
        ((4, 2, 32, HALF), BF16), ((4, 2, 32, HALF), BF16), ((4, 32, HALF), BF16),
        ((4, 2, 2, 32, 640), BF16),
        ((2, 4, 2, 32, 128), BF16), ((2, 4, 32, 128), BF16), ((2, 4, 32, 128), BF16),
        ((4, 32, 128), BF16), ((4, 4, 32, 128), BF16), ((128, 128), F32), ((4, 32, 128), BF16),
        ((2, 6656), F32), ((56, 256), F32), ((16, 256), F32), ((2, 6144), F32), ((128, 128), F32),
        ((2, 4, 32, 128), BF16), ((4, 64, 128), BF16), ((2, 4, 64, 128), BF16),
        ((4, 128, 128), BF16), ((4, 128, 128), BF16), ((512, 128), BF16),
        ((128, 512), BF16), ((512, 512), BF16), ((512, 512), BF16),
        ((256, WIDTH), F32), ((4, 4, 4, 16, HALF), BF16), ((4, 6, 2, 16, HALF), BF16),
        ((4, 2, 2, 16, HALF), BF16), ((4, 4, 16, HALF), BF16),
        ((4, 3, 16, HALF), BF16), ((3, 16, HALF), BF16), ((3, 16, HALF), BF16),
        128, 128,
    ]
    return pl.pallas_call(
        kernel,
        name="layer",
        out_shape=jax.ShapeDtypeStruct((2, 4, WIDTH), BF16),
        in_specs=[pl.BlockSpec(memory_space=pltpu.SMEM)] + [far] * 8,
        out_specs=pl.BlockSpec(memory_space=pltpu.VMEM),
        scratch_shapes=[
            pltpu.SemaphoreType.DMA((entry,)) if isinstance(entry, int) else pltpu.VMEM(*entry)
            for entry in scratch
        ],
        compiler_params=pltpu.CompilerParams(
            collective_id=0, has_side_effects=True, vmem_limit_bytes=56 * 2**20 - 160 * 2**10
        ),
    )(
        lengths, hidden_in, norm_gain, w_qkv.T, w_gate.T, w_up.T,
        w_out, w_down, kv_cache,
    )


def solution(mesh):
    return jax.shard_map(
        per_device,
        mesh=mesh,
        in_specs=(
            P(None, "yz", "gx"),
            P("gx"),
            P("gx", "yz"),
            P("gx", "yz"),
            P("gx", "yz"),
            P("yz", "gx"),
            P("yz", "gx"),
            P(("gx", "yz"), None, None),
            P(("gx", "yz")),
        ),
        out_specs=P(None, "yz", "gx"),
        check_vma=False,
    )
```
